512 devices in a mesh: gx: 8 (over x, core), gy: 4 (over y), gz: 16 (over z).
Axes of the slice: x: 4, y: 4, z: 16, core: 2. Of those that a mesh axis runs over, the one named last changes fastest.
Arguments:
- probes: bfloat16 [48, 3, 8, 8, 2048], P(None, None, 'gx', 'gy', 'gz'), may hold values from -6 to 6
- stiffness: float32 [8, 8, 2048], P('gx', 'gy', 'gz'), may hold values from 0.1 to 10
- diag_tiles: bfloat16 [8, 4, 16, 6, 128, 128], P('gx', 'gy', 'gz'), may hold values from -0.25 to 3.25
- off_tiles: bfloat16 [8, 4, 16, 24, 128, 128], P('gx', 'gy', 'gz'), may hold values from -0.3984375 to 0.3984375
- off_rows: int32 [8, 4, 16, 24], P('gx', 'gy', 'gz'), may hold values from 0 to 5
- off_cols: int32 [8, 4, 16, 24], P('gx', 'gy', 'gz'), may hold values from 0 to 5
- off_count: int32 [8, 4, 16], P('gx', 'gy', 'gz'), may hold values from 12 to 24, as said below
Outputs:
- deflation: bfloat16 [32, 3, 8, 8, 2048], P(None, None, 'gx', 'gy', 'gz')
- coarse_self: float32 [8, 4, 16, 1024], P('gx', 'gy')
- coarse_pairs: float32 [8, 4, 16, 26, 1024], P('gx', 'gy')
The draws below stay inside these ranges and needn't reach their ends.
Inputs may be any that keep to these rules, and one draw needn't show every extreme that they name: `off_count`: some subdomain has exactly 24 tiles in use.
All inputs are finite; a program needn't handle non-finite values.
Results may differ from the reference program's by a relative error of at most 0.0051.
Values may be sent and summed in bfloat16 or wider, within the bound.
A program may use at most 64 MiB of HBM per device.

```python
import math
import jax
import jax.numpy as jnp
from jax import lax

CX = 1
CY = 2
CZ = 128
MAXT = 24
PROBES = 48
DEFL = 32
ITERS = 12
RT = 6
ROWS = 768
NX = 8
NY = 8
NZ = 2048
N_GX = 8
N_GY = 4
N_GZ = 16


def draw_diag_tiles(key, part):
    key = jax.random.fold_in(key, 11)
    noise_key, level_key = jax.random.split(key)
    shape = (N_GX, N_GY, N_GZ, RT, CZ, CZ)
    noise = 0.05 * jax.random.normal(noise_key, shape, jnp.float32)
    levels = jax.random.uniform(level_key, (N_GX, N_GY, N_GZ, RT, CZ, 1), jnp.float32, 1.0, 3.25)
    identity = (jnp.arange(CZ)[:, None] == jnp.arange(CZ)[None, :]).astype(jnp.float32)
    tiles = jnp.clip(noise, -0.25, 0.25) + levels * identity
    return jnp.clip(tiles, -0.25, 3.25).astype(jnp.bfloat16)


def draw_off_count(key, part):
    key = jax.random.fold_in(key, 23)
    count_key, peak_key = jax.random.split(key)
    device_count = N_GX * N_GY * N_GZ
    counts = jax.random.randint(count_key, (N_GX, N_GY, N_GZ), MAXT // 2, MAXT + 1, dtype=jnp.int32)
    peak_device = jax.random.randint(peak_key, (), 0, device_count, dtype=jnp.int32)
    flat_index = jnp.arange(device_count, dtype=jnp.int32).reshape(N_GX, N_GY, N_GZ)
    return jnp.where(flat_index == peak_device, jnp.int32(MAXT), counts).astype(jnp.int32)


def touch_ends(array, key, least, high):
    index_at = [jax.random.randint(jax.random.fold_in(key, axis), (), 0, length) for axis, length in enumerate(array.shape)]
    longest = array.shape.index(max(array.shape))
    next_to = index_at[:longest] + [(index_at[longest] + 1) % array.shape[longest]] + index_at[longest + 1:]
    return array.at[tuple(index_at)].set(least).at[tuple(next_to)].set(high)


def shard_levels(rng, extent, shards, low, largest):
    loudness, own = 1.0, jax.random.fold_in(rng, 6)
    for axis_at, parts in shards:
        draws = jnp.exp(jax.random.uniform(jax.random.fold_in(own, axis_at), (parts,), jnp.float32, low / len(shards), largest / len(shards)))
        loudness = loudness * jnp.repeat(draws, extent[axis_at] // parts).reshape([-1 if axis == axis_at else 1 for axis in range(len(extent))])
    return loudness


def bell_draw(rng, shape, deviation, most, shards=(), held_as=jnp.bfloat16):
    values = jax.random.normal(rng, shape, jnp.float32) * deviation
    if len(shards) > 0:
        values = shard_levels(rng, shape, shards, -0.22, 0.18) * values
    return jnp.clip(values, min=-most, max=most).astype(held_as)


def setup_inputs(seed: int = 0) -> dict:
    key_of = jax.random.split(jax.random.key(seed), 8)
    return {
        "probes": bell_draw(key_of[0], (PROBES, 3, NX, NY, NZ), 1.0, 6.0, ((2, 8), (3, 4), (4, 16))),
        "stiffness": jnp.clip(jnp.exp(math.log(10.0) - 4.6051702 * jax.random.uniform(key_of[1], (NX, NY, NZ), jnp.float32) ** shard_levels(key_of[1], (NX, NY, NZ), ((0, 8), (1, 4), (2, 16)), -0.2, 0.2)), 0.1, 10.0),
        "diag_tiles": draw_diag_tiles(jax.random.fold_in(key_of[7], 71), 0),
        "off_tiles": bell_draw(key_of[3], (N_GX, N_GY, N_GZ, MAXT, CZ, CZ), 0.05, 0.3984375, ((0, 8), (1, 4), (2, 16))),
        "off_rows": touch_ends(jax.random.randint(key_of[4], (N_GX, N_GY, N_GZ, MAXT), 0, RT), jax.random.fold_in(key_of[4], 1), 0, RT - 1).astype(jnp.int32),
        "off_cols": touch_ends(jax.random.randint(key_of[5], (N_GX, N_GY, N_GZ, MAXT), 0, RT), jax.random.fold_in(key_of[5], 1), 0, RT - 1).astype(jnp.int32),
        "off_count": draw_off_count(jax.random.fold_in(key_of[7], 71), 0),
    }


spectral_shift = 8.0

def tile_apply(vectors, diagonal, off_block, tile_rows, tile_cols, tile_count):
    result = jnp.einsum('tij,ktj->kti', diagonal.astype(jnp.float32), vectors.astype(jnp.float32))
    picked = vectors[:, tile_cols, :]
    product = jnp.einsum('mij,kmj->kmi', off_block.astype(jnp.float32), picked.astype(jnp.float32))
    live_mask = jnp.arange(off_block.shape[0], dtype=jnp.int32) < tile_count
    product = jnp.where(live_mask[None, :, None], product, jnp.zeros_like(product))
    return result.at[:, tile_rows, :].add(product)

def sketch(probe_block, weight_rows, diagonal, off_block, tile_rows, tile_cols, tile_count):
    probe_count = probe_block.shape[0]
    basis = probe_block.astype(jnp.float32).reshape(probe_count, ROWS)
    for iteration in range(ITERS):
        scaled = (basis * weight_rows).astype(jnp.bfloat16).reshape(probe_count, RT, CZ)
        applied = tile_apply(scaled, diagonal, off_block, tile_rows, tile_cols, tile_count).reshape(probe_count, ROWS)
        image = spectral_shift * basis - weight_rows * applied
        gram_matrix = jnp.dot(image, image.T, precision=lax.Precision.HIGHEST) / ROWS
        lower_factor = jnp.linalg.cholesky(gram_matrix)
        basis = lax.linalg.triangular_solve(lower_factor, image, left_side=True, lower=True)
    return basis

def rim_span(offset, length):
    if offset < 0:
        return (0, 1, 0)
    if offset == 0:
        return (0, length, 1)
    return (length - 1, 1, length + 1)

def couplings(field, extended):
    blocks = []
    length_x, length_y, length_z = field.shape[2:]
    for offset_x in (-1, 0, 1):
        for offset_y in (-1, 0, 1):
            for offset_z in (-1, 0, 1):
                if offset_x == 0 and offset_y == 0 and (offset_z == 0):
                    continue
                own_x, span_x, ext_x = rim_span(offset_x, length_x)
                own_y, span_y, ext_y = rim_span(offset_y, length_y)
                own_z, span_z, ext_z = rim_span(offset_z, length_z)
                own_part = field[:, :, own_x:own_x + span_x, own_y:own_y + span_y, own_z:own_z + span_z]
                ext_part = extended[:, :, ext_x:ext_x + span_x, ext_y:ext_y + span_y, ext_z:ext_z + span_z]
                blocks.append(-jnp.einsum('kcxyz,lcxyz->kl', own_part.astype(jnp.float32), ext_part.astype(jnp.float32)))
    return jnp.stack(blocks)

def reference(probes, stiffness, diag_tiles, off_tiles, off_rows, off_cols, off_count):
    padded = jnp.pad(stiffness, 1)
    neighbour_sum = padded[2:, 1:-1, 1:-1] + padded[:-2, 1:-1, 1:-1]
    neighbour_sum = neighbour_sum + padded[1:-1, 2:, 1:-1] + padded[1:-1, :-2, 1:-1]
    neighbour_sum = neighbour_sum + padded[1:-1, 1:-1, 2:] + padded[1:-1, 1:-1, :-2]
    weight = stiffness / (stiffness + neighbour_sum / 6.0)
    device_count = N_GX * N_GY * N_GZ
    probe_dev = probes.reshape(PROBES, 3, N_GX, CX, N_GY, CY, N_GZ, CZ).transpose(2, 4, 6, 0, 1, 3, 5, 7).reshape(device_count, PROBES, 3, CX, CY, CZ)
    weight_dev = weight.reshape(N_GX, CX, N_GY, CY, N_GZ, CZ).transpose(0, 2, 4, 1, 3, 5).reshape(device_count, CX, CY, CZ)
    diag_dev = diag_tiles.reshape(device_count, RT, CZ, CZ)
    off_dev = off_tiles.reshape(device_count, MAXT, CZ, CZ)
    rows_dev = off_rows.reshape(device_count, MAXT)
    cols_dev = off_cols.reshape(device_count, MAXT)
    count_dev = off_count.reshape(device_count)

    def one_subdomain(operands):
        probe_block, weight_block, diagonal, off_block, tile_rows, tile_cols, tile_count = operands
        weight_rows = jnp.broadcast_to(weight_block[None], (3, CX, CY, CZ)).reshape(ROWS)
        basis = sketch(probe_block, weight_rows, diagonal, off_block, tile_rows, tile_cols, tile_count)
        kept = basis[:DEFL]
        weighted = (kept * weight_rows).astype(jnp.bfloat16)
        applied = tile_apply(weighted.reshape(DEFL, RT, CZ), diagonal, off_block, tile_rows, tile_cols, tile_count).reshape(DEFL, ROWS)
        self_block = jnp.dot(weighted.astype(jnp.float32), applied.T, precision=lax.Precision.HIGHEST) / ROWS
        return (kept.astype(jnp.bfloat16), weighted, self_block)
    kept_dev, weighted_dev, self_dev = lax.map(one_subdomain, (probe_dev, weight_dev, diag_dev, off_dev, rows_dev, cols_dev, count_dev))
    deflation = kept_dev.reshape(N_GX, N_GY, N_GZ, DEFL, 3, CX, CY, CZ).transpose(3, 4, 0, 5, 1, 6, 2, 7).reshape(DEFL, 3, NX, NY, NZ)
    field_all = weighted_dev.reshape(N_GX, N_GY, N_GZ, DEFL, 3, CX, CY, CZ).transpose(3, 4, 0, 5, 1, 6, 2, 7).reshape(DEFL, 3, NX, NY, NZ)
    field_pad = jnp.pad(field_all, ((0, 0), (0, 0), (1, 1), (1, 1), (1, 1)))

    def pairs_of(device_index):
        grid_x = device_index // (N_GY * N_GZ)
        grid_y = device_index // N_GZ % N_GY
        grid_z = device_index % N_GZ
        zero_index = jnp.int32(0)
        starts = (zero_index, zero_index, (grid_x * CX).astype(jnp.int32), (grid_y * CY).astype(jnp.int32), (grid_z * CZ).astype(jnp.int32))
        own_field = lax.dynamic_slice(field_all, starts, (DEFL, 3, CX, CY, CZ))
        ext_field = lax.dynamic_slice(field_pad, starts, (DEFL, 3, CX + 2, CY + 2, CZ + 2))
        return couplings(own_field, ext_field)
    pair_dev = lax.map(pairs_of, jnp.arange(device_count, dtype=jnp.int32))
    coarse_self = self_dev.reshape(N_GX, N_GY, N_GZ, DEFL * DEFL)
    coarse_pairs = pair_dev.reshape(N_GX, N_GY, N_GZ, 26, DEFL * DEFL)
    return (deflation, coarse_self, coarse_pairs)
```

```python
import jax
import jax.numpy as jnp
from jax import lax
from jax.experimental import pallas as pl
from jax.experimental.pallas import tpu as pltpu
from jax.sharding import PartitionSpec as P

MESH = pl.DeviceIdType.MESH
F32 = jnp.float32
BF16 = jnp.bfloat16
HIGHEST = lax.Precision.HIGHEST

DEFL = 32
ITERS = 12
SHIFT = 8.0
TILE = 128
SAFE_PIVOT = 0.01


def iota(shape, dim):
    return lax.broadcasted_iota(jnp.int32, shape, dim)


def dot_nt(a, b, precision=None):
    return lax.dot_general(
        a, b, (((1,), (1,)), ((), ())), preferred_element_type=F32, precision=precision
    )


def weight_kernel(stiff_ref, weight_ref, got, send_sem, recv_sem):
    sizes = [lax.axis_size(a) for a in ("gx", "gy", "gz")]
    here = [lax.axis_index(a) for a in ("gx", "gy", "gz")]
    faces = []
    for dim, size in enumerate(sizes):
        for step in (-1, 1):
            there = list(here)
            there[dim] = lax.rem(here[dim] + step + size, size)
            faces.append(tuple(there))
    barrier = pltpu.get_barrier_semaphore()
    for there in faces:
        pl.semaphore_signal(barrier, inc=1, device_id=there, device_id_type=MESH)
    pl.semaphore_wait(barrier, len(faces))
    copies = []
    for face, there in enumerate(faces):
        copy = pltpu.make_async_remote_copy(
            src_ref=stiff_ref,
            dst_ref=got.at[face ^ 1],
            send_sem=send_sem.at[face],
            recv_sem=recv_sem.at[face ^ 1],
            device_id=there,
            device_id_type=MESH,
        )
        copy.start()
        copies.append(copy)
    for copy in copies:
        copy.wait()
    zero = jnp.zeros(stiff_ref.shape, F32)
    stiff = stiff_ref[...]

    def face_value(face):
        dim, high = face // 2, face % 2
        inside = here[dim] < sizes[dim] - 1 if high else here[dim] > 0
        return jnp.where(inside, got[face], zero)

    total = face_value(1) + face_value(0)
    row = iota(stiff.shape, 0)
    y_low, y_high = face_value(2), face_value(3)
    total = total + jnp.where(row == 0, pltpu.roll(stiff, 1, 0), y_high[0:1, :])
    total = total + jnp.where(row == 1, pltpu.roll(stiff, 1, 0), y_low[1:2, :])
    lane = iota(stiff.shape, 1)
    z_low, z_high = face_value(4), face_value(5)
    width = stiff.shape[1]
    total = total + jnp.where(
        lane == width - 1, z_high[:, 0:1], pltpu.roll(stiff, width - 1, 1)
    )
    total = total + jnp.where(lane == 0, z_low[:, width - 1 : width], pltpu.roll(stiff, 1, 1))
    weight_ref[...] = stiff / (stiff + total / 6.0)


def cell_weights(stiff):
    return pl.pallas_call(
        weight_kernel,
        out_shape=jax.ShapeDtypeStruct(stiff.shape, F32),
        in_specs=[pl.BlockSpec(memory_space=pltpu.VMEM)],
        out_specs=pl.BlockSpec(memory_space=pltpu.VMEM),
        scratch_shapes=[
            pltpu.VMEM((6,) + stiff.shape, F32),
            pltpu.SemaphoreType.DMA((6,)),
            pltpu.SemaphoreType.DMA((6,)),
        ],
        compiler_params=pltpu.CompilerParams(collective_id=0, has_side_effects=True),
        name="cell_weights",
    )(stiff)


def eliminate(gram):
    count = gram.shape[0]
    start = jnp.concatenate([gram, (iota(gram.shape, 0) == iota(gram.shape, 1)).astype(F32)], 1)
    row = iota((count, 1), 0)
    work = start
    pivots = jnp.zeros((count, 1), F32)
    for j in range(count):
        column = work[:, j : j + 1]
        pivot = column[j : j + 1, :]
        factor = jnp.where(row > j, column * (1.0 / pivot), 0.0)
        pivots = jnp.where(row == j, column, pivots)
        work = work - factor * work[j : j + 1, :]
    inverse = work[:, count:] * lax.rsqrt(pivots)
    original = jnp.sum(
        jnp.where(iota(gram.shape, 0) == iota(gram.shape, 1), gram, 0.0), axis=1, keepdims=True
    )
    return inverse, jnp.min(pivots / original)


def split(x):
    high = x.astype(BF16)
    return high, (x - high.astype(F32)).astype(BF16)


def basis_kernel(
    rows_ref, cols_ref, count_ref, probe_ref, weight_ref, diag_ref, off_ref,
    defl_ref, field_ref, self_ref,
    dense, matrix,
):
    tiles = diag_ref.shape[0]
    total = tiles * TILE
    probes = probe_ref.shape[0]
    eye = iota((TILE, TILE), 0) == iota((TILE, TILE), 1)

    dense[...] = jnp.zeros(dense.shape, F32)
    for t in range(tiles):
        dense[t, t] = diag_ref[t].astype(F32)

    def add_tile(m, carry):
        t, u = rows_ref[m], cols_ref[m]
        dense[t, u] = dense[t, u] + off_ref[m].astype(F32)
        return carry

    lax.fori_loop(0, count_ref[0], add_tile, 0)
    level = []
    for t in range(tiles):
        for u in range(tiles):
            block = dense[t, u]
            if t == u:
                level.append(jnp.sum(jnp.where(eye, block, 0.0), axis=0, keepdims=True))
                block = jnp.where(eye, 0.0, block)
            matrix[u * TILE : (u + 1) * TILE, t * TILE : (t + 1) * TILE] = block.T.astype(BF16)
    level = jnp.concatenate(level, axis=1)
    weight = weight_ref[...]
    weight = jnp.concatenate([weight[0:1, :], weight[1:2, :]] * (tiles // 2), axis=1)
    step_weight = weight * (1.0 / SHIFT)

    def apply(high, low):
        both = jnp.dot(
            jnp.concatenate([high, low], axis=0), matrix[...], preferred_element_type=F32
        )
        return both[: high.shape[0]] + both[high.shape[0] :]

    def image_of(basis):
        scaled = basis * weight
        return basis - step_weight * (apply(*split(scaled)) + level * scaled)

    def normaliser(image):
        return eliminate(dot_nt(image, image, HIGHEST) * (1.0 / total))

    def finish(inverse, image):
        kept = jnp.dot(inverse, image, preferred_element_type=F32, precision=HIGHEST)[:DEFL]
        defl_ref[...] = kept.astype(BF16)
        weighted = (kept * weight).astype(BF16)
        for t in range(tiles):
            field_ref[t % 2, :, t // 2 * TILE : (t // 2 + 1) * TILE] = weighted[
                :, t * TILE : (t + 1) * TILE
            ]
        wide = weighted.astype(F32)
        applied = jnp.dot(weighted, matrix[...], preferred_element_type=F32) + level * wide
        high, low = split(applied)
        self_ref[...] = (dot_nt(weighted, high) + dot_nt(weighted, low)) * (1.0 / total)

    image = probe_ref[...].astype(F32)
    for _ in range(ITERS):
        image = image_of(image)
    inverse, least = normaliser(image)
    finish(inverse, image)

    @pl.when(jnp.logical_not(least > SAFE_PIVOT))
    def _():
        def iteration(_, basis):
            image = image_of(basis)
            inverse, _ = normaliser(image)
            return jnp.dot(inverse, image, preferred_element_type=F32, precision=HIGHEST)

        basis = lax.fori_loop(0, ITERS - 1, iteration, probe_ref[...].astype(F32))
        image = image_of(basis)
        inverse, _ = normaliser(image)
        finish(inverse, image)


def local_basis(probes, weight, diagonal, off_block, rows, cols, count):
    tiles = diagonal.shape[0]
    total = tiles * TILE
    smem = pl.BlockSpec(memory_space=pltpu.SMEM)
    vmem = pl.BlockSpec(memory_space=pltpu.VMEM)
    return pl.pallas_call(
        basis_kernel,
        out_shape=(
            jax.ShapeDtypeStruct((DEFL, total), BF16),
            jax.ShapeDtypeStruct((2, DEFL, total // 2), BF16),
            jax.ShapeDtypeStruct((DEFL, DEFL), F32),
        ),
        in_specs=[smem, smem, smem, vmem, vmem, vmem, vmem],
        out_specs=(vmem, vmem, vmem),
        scratch_shapes=[
            pltpu.VMEM((tiles, tiles, TILE, TILE), F32),
            pltpu.VMEM((total, total), BF16),
        ],
        compiler_params=pltpu.CompilerParams(vmem_limit_bytes=24 * 2**20),
        name="local_basis",
    )(rows, cols, count, probes, weight, diagonal, off_block)


PLANE = 9
OWN = 4
PARTS = 16
PAYLOAD_ROWS = 16


def plane_step(m):
    return m // 3 - 1, m % 3 - 1


def end_picker(y, half):
    row, lane = iota((PARTS, half), 0), iota((PARTS, half), 1)
    end, part = row // 8, row % 8
    hit = (part // 3 == y) & (part < 6) & (lane == (part % 3) * TILE + end * (TILE - 1))
    return hit.astype(BF16)


def exchange_kernel(
    field_ref, self_ref, out_ref, full, sides, ring, send_sem, recv_sem, up_send, up_recv,
    down_send, down_recv,
):
    n_x, n_y, n_z = (lax.axis_size(a) for a in ("gx", "gy", "gz"))
    my_x, my_y, my_z = (lax.axis_index(a) for a in ("gx", "gy", "gz"))
    half = field_ref.shape[2]

    def device(m):
        step_x, step_y = plane_step(m)
        return (lax.rem(my_x + step_x + n_x, n_x), lax.rem(my_y + step_y + n_y, n_y), my_z)

    def line(step):
        return (my_x, my_y, lax.rem(my_z + step + n_z, n_z))

    neighbours = [m for m in range(PLANE) if m != OWN]
    barrier = pltpu.get_barrier_semaphore()
    for m in neighbours:
        pl.semaphore_signal(barrier, inc=1, device_id=device(m), device_id_type=MESH)
    for step in (-1, 1):
        pl.semaphore_signal(barrier, inc=1, device_id=line(step), device_id_type=MESH)
    pl.semaphore_wait(barrier, len(neighbours) + 2)

    slot = {m: i for i, m in enumerate(m for m in neighbours if plane_step(m)[1] != 0)}
    copies = []
    for m in neighbours:
        step_x, step_y = plane_step(m)
        back = PLANE - 1 - m
        if step_y == 0:
            source, target = field_ref, full.at[back // 3 // 2]
        else:
            source, target = field_ref.at[1 if step_y > 0 else 0], sides.at[slot[back]]
        copy = pltpu.make_async_remote_copy(
            src_ref=source,
            dst_ref=target,
            send_sem=send_sem.at[m],
            recv_sem=recv_sem.at[back],
            device_id=device(m),
            device_id_type=MESH,
        )
        copy.start()
        copies.append(copy)

    pick = [end_picker(y, half) for y in range(2)]
    own = [field_ref[y] for y in range(2)]
    stack = [[jnp.concatenate([-own[y], pick[z]], axis=0) for z in range(2)] for y in range(2)]
    spread = (iota((DEFL, DEFL * DEFL), 1) % DEFL == iota((DEFL, DEFL * DEFL), 0)).astype(BF16)
    for copy in copies:
        copy.wait_recv()

    parts = []
    for m in range(PLANE):
        step_x, step_y = plane_step(m)
        if m == OWN:
            ends = dot_nt(pick[0], own[0]) + dot_nt(pick[1], own[1])
            parts.append(jnp.concatenate([self_ref[...], ends], axis=0))
            continue
        if step_y == 0:
            side = m // 3 // 2
            block = dot_nt(stack[0][0], full[side, 0]) + dot_nt(stack[1][1], full[side, 1])
        elif step_y < 0:
            block = dot_nt(stack[0][1], sides[slot[m]])
        else:
            block = dot_nt(stack[1][0], sides[slot[m]])
        inside = True
        if step_x != 0:
            inside = my_x < n_x - 1 if step_x > 0 else my_x > 0
        if step_y != 0:
            inside = jnp.logical_and(inside, my_y < n_y - 1 if step_y > 0 else my_y > 0)
        parts.append(jnp.where(inside, block, 0.0))
    parts = jnp.concatenate(parts, axis=0).astype(BF16)

    group = DEFL + PARTS
    rows = PLANE * group
    wide = jnp.dot(parts, spread, preferred_element_type=F32)
    row = iota((rows, 1), 0)
    m, r = row // group, row % group
    place = jnp.where(r < DEFL, r, (PARTS * m + r - DEFL) % DEFL)
    lane_group = iota((rows, DEFL * DEFL), 1) // DEFL
    wide = jnp.where(lane_group == place, wide, 0.0).astype(BF16)
    column = iota((PAYLOAD_ROWS, rows), 1)
    m, r = column // group, column % group
    target = jnp.where(r < DEFL, m, PLANE + (PARTS * m + r - DEFL) // DEFL)
    gather = (target == iota((PAYLOAD_ROWS, rows), 0)).astype(BF16)
    ring[my_z] = jnp.dot(gather, wide, preferred_element_type=F32).astype(BF16)

    steps_up = n_z // 2
    steps_down = n_z - 1 - steps_up

    def hop(owner, step, sends, recvs, t):
        return pltpu.make_async_remote_copy(
            src_ref=ring.at[owner],
            dst_ref=ring.at[owner],
            send_sem=sends.at[t],
            recv_sem=recvs.at[t],
            device_id=line(step),
            device_id_type=MESH,
        )

    hops = []
    for t in range(steps_up):
        up = hop(lax.rem(my_z - t + n_z, n_z), 1, up_send, up_recv, t)
        up.start()
        hops.append(up)
        if t < steps_down:
            down = hop(lax.rem(my_z + t, n_z), -1, down_send, down_recv, t)
            down.start()
            hops.append(down)
        up.wait_recv()
        if t < steps_down:
            down.wait_recv()
    for copy in copies + hops:
        copy.wait_send()
    out_ref[...] = ring[...]


def exchange(field, self_block, n_z):
    vmem = pl.BlockSpec(memory_space=pltpu.VMEM)
    dma = pltpu.SemaphoreType.DMA
    half = field.shape[2]
    payload = (n_z, PAYLOAD_ROWS, DEFL * DEFL)
    return pl.pallas_call(
        exchange_kernel,
        out_shape=jax.ShapeDtypeStruct(payload, BF16),
        in_specs=[vmem, vmem],
        out_specs=vmem,
        scratch_shapes=[
            pltpu.VMEM((2, 2, DEFL, half), BF16),
            pltpu.VMEM((6, DEFL, half), BF16),
            pltpu.VMEM(payload, BF16),
            dma((PLANE,)),
            dma((PLANE,)),
            dma((n_z // 2,)),
            dma((n_z // 2,)),
            dma((n_z // 2,)),
            dma((n_z // 2,)),
        ],
        compiler_params=pltpu.CompilerParams(
            collective_id=1, has_side_effects=True, vmem_limit_bytes=24 * 2**20
        ),
        name="exchange",
    )(field, self_block)


def pair_index(m, step_z):
    flat = 3 * m + step_z + 1
    return flat if flat < 13 else flat - 1


def unpack_kernel(gathered_ref, self_ref, pairs_ref):
    n_z = self_ref.shape[0]
    width = DEFL * DEFL
    packed = gathered_ref[...]
    cells = n_z * PAYLOAD_ROWS
    column = iota((1, cells), 1)

    def select(rows, shift):
        index = iota((len(rows) * n_z, 1), 0)
        member = index % n_z + shift
        wanted = jnp.full(index.shape, rows[0], jnp.int32)
        for i in range(1, len(rows)):
            wanted = jnp.where(index // n_z == i, rows[i], wanted)
        inside = (member >= 0) & (member < n_z)
        wanted = jnp.where(inside, member * PAYLOAD_ROWS + wanted, -1)
        hit = (column == wanted).astype(BF16)
        return jnp.dot(hit, packed, preferred_element_type=F32)

    blocks = select(list(range(PLANE)), 0)
    for m in range(PLANE):
        block = blocks[m * n_z : (m + 1) * n_z]
        if m == OWN:
            self_ref[...] = block
        else:
            pairs_ref[pair_index(m, 0)] = block

    per_tile = TILE // DEFL
    own_row = PLANE + OWN * PARTS // DEFL
    own_tiles = select([own_row], 0).astype(BF16)
    own_tiles = jnp.concatenate(
        [own_tiles[:, i * TILE : (i + 1) * TILE] for i in range(PARTS // per_tile)], axis=0
    )
    value, lane = iota((TILE, width), 0), iota((TILE, width), 1)
    own = []
    for v in range(per_tile):
        spread = jnp.where(value == v * DEFL + lane // DEFL, -1.0, 0.0).astype(BF16)
        own.append(jnp.dot(own_tiles, spread, preferred_element_type=F32))

    def own_part(part):
        i = part // per_tile
        return own[part % per_tile][i * n_z : (i + 1) * n_z]

    value, lane = iota((TILE, per_tile * TILE), 0), iota((TILE, per_tile * TILE), 1)
    repeat = (value == lane // TILE * DEFL + lane % DEFL).astype(BF16)
    end_rows = list(range(PLANE, PLANE + (PLANE * PARTS + DEFL - 1) // DEFL))
    for step_z in (-1, 1):
        rows = select(end_rows, step_z).astype(BF16)
        first = 0 if step_z > 0 else 2
        tiles = [first, first + 1, first + 4, first + 5]
        stacked = jnp.concatenate([rows[:, i * TILE : (i + 1) * TILE] for i in tiles], axis=0)
        theirs = jnp.dot(stacked, repeat, preferred_element_type=F32)

        def their_part(m, part):
            block = (m % 2) * 2 + part // per_tile
            start = (block * len(end_rows) + m // 2) * n_z
            v = part % per_tile
            return theirs[start : start + n_z, v * TILE : (v + 1) * TILE]

        own_end = 8 if step_z > 0 else 0
        for m in range(PLANE):
            step_y = plane_step(m)[1]
            pairs = [(0, 0), (1, 1)] if step_y == 0 else [(0, 1)] if step_y < 0 else [(1, 0)]
            total = None
            for own_y, their_y in pairs:
                for c in range(3):
                    left = own_part(own_end + own_y * 3 + c)
                    right = jnp.concatenate([their_part(m, their_y * 3 + c)] * (width // TILE), 1)
                    term = left * right
                    total = term if total is None else total + term
            pairs_ref[pair_index(m, step_z)] = total


def unpack(gathered, n_z):
    vmem = pl.BlockSpec(memory_space=pltpu.VMEM)
    width = DEFL * DEFL
    return pl.pallas_call(
        unpack_kernel,
        out_shape=(
            jax.ShapeDtypeStruct((n_z, width), F32),
            jax.ShapeDtypeStruct((26, n_z, width), F32),
        ),
        in_specs=[vmem],
        out_specs=(vmem, vmem),
        compiler_params=pltpu.CompilerParams(vmem_limit_bytes=32 * 2**20),
        name="unpack",
    )(gathered.reshape(n_z * PAYLOAD_ROWS, width))


def per_device(probes, stiffness, diag_tiles, off_tiles, off_rows, off_cols, off_count):
    n_z = lax.axis_size("gz")
    cell_shape = probes.shape[1:]
    weight = cell_weights(stiffness[0])
    deflation, field, self_block = local_basis(
        probes.reshape(probes.shape[0], -1),
        weight,
        diag_tiles[0, 0, 0],
        off_tiles[0, 0, 0],
        off_rows[0, 0, 0],
        off_cols[0, 0, 0],
        off_count[0, 0],
    )
    gathered = exchange(field, self_block, n_z)
    coarse_self, coarse_pairs = unpack(gathered, n_z)
    return (
        deflation.reshape((DEFL,) + cell_shape),
        coarse_self[None, None],
        coarse_pairs.transpose(1, 0, 2)[None, None],
    )


def solution(mesh):
    placed = (
        P(None, None, "gx", "gy", "gz"),
        P("gx", "gy", "gz"),
        P("gx", "gy", "gz", None, None, None),
        P("gx", "gy", "gz", None, None, None),
        P("gx", "gy", "gz", None),
        P("gx", "gy", "gz", None),
        P("gx", "gy", "gz"),
    )
    return jax.shard_map(
        per_device,
        mesh=mesh,
        in_specs=placed,
        out_specs=(
            P(None, None, "gx", "gy", "gz"),
            P("gx", "gy", None, None),
            P("gx", "gy", None, None, None),
        ),
        check_vma=False,
    )
```

```python
import jax
import jax.numpy as jnp
from jax import lax
from jax.experimental import pallas as pl
from jax.experimental.pallas import tpu as pltpu
from jax.sharding import PartitionSpec as P

MESH = pl.DeviceIdType.MESH
F32 = jnp.float32
BF16 = jnp.bfloat16
HIGHEST = lax.Precision.HIGHEST

DEFL = 32
ITERS = 12
SHIFT = 8.0
TILE = 128
SAFE_PIVOT = 0.01


def iota(shape, dim):
    return lax.broadcasted_iota(jnp.int32, shape, dim)


def dot_nt(a, b, precision=None):
    return lax.dot_general(
        a, b, (((1,), (1,)), ((), ())), preferred_element_type=F32, precision=precision
    )


def operands_kernel(
    stiff_hbm, rows_hbm, cols_hbm, count_hbm, probe_hbm, diag_hbm, off_hbm,
    weight_ref, basis_ref, level_ref, matrix_ref,
    got, stiff_ref, rows_ref, cols_ref, count_ref, key_ref, probe_ref, diag_ref, off_ref, wide, sums,
    send_sem, recv_sem, local_sem,
):
    sizes = [lax.axis_size(a) for a in ("gx", "gy", "gz")]
    here = [lax.axis_index(a) for a in ("gx", "gy", "gz")]
    slots, tiles = off_ref.shape[0], diag_ref.shape[0]
    faces = []
    for dim, size in enumerate(sizes):
        for step in (-1, 1):
            there = list(here)
            there[dim] = lax.rem(here[dim] + step + size, size)
            faces.append(tuple(there))
    barrier = pltpu.get_barrier_semaphore()
    for there in faces:
        pl.semaphore_signal(barrier, inc=1, device_id=there, device_id_type=MESH)
    loads = []
    for source, target in (
        (rows_hbm, rows_ref),
        (cols_hbm, cols_ref),
        (count_hbm, count_ref),
        (off_hbm, off_ref),
        (diag_hbm, diag_ref),
        (probe_hbm, probe_ref),
        (stiff_hbm, stiff_ref),
    ):
        load = pltpu.make_async_copy(source, target, local_sem.at[len(loads)])
        load.start()
        loads.append(load)
    pl.semaphore_wait(barrier, len(faces))
    copies = []
    for face, there in enumerate(faces):
        copy = pltpu.make_async_remote_copy(
            src_ref=stiff_hbm,
            dst_ref=got.at[face ^ 1],
            send_sem=send_sem.at[face],
            recv_sem=recv_sem.at[face ^ 1],
            device_id=there,
            device_id_type=MESH,
        )
        copy.start()
        copies.append(copy)

    for load in loads[:3]:
        load.wait()
    count = count_ref[0]
    for m in range(slots):
        key_ref[m] = jnp.where(m < count, rows_ref[m] * tiles + cols_ref[m], -1 - m)
    sums[slots] = jnp.zeros((TILE, TILE), F32)
    loads[3].wait()

    def add_tile(m, carry):
        key, before = key_ref[m], slots
        for other in range(slots - 1):
            before = jnp.where((other < m) & (key_ref[other] == key), other, before)
        sums[m] = off_ref[m].astype(F32) + sums[before]
        return carry

    lax.fori_loop(0, slots, add_tile, 0)

    def dense_block(place):
        last = slots
        for m in range(slots):
            last = jnp.where(key_ref[m] == place, m, last)
        return sums[last]

    for t in range(tiles):

        def put(u, carry, t=t):
            rows = pl.ds(pl.multiple_of(u * TILE, TILE), TILE)
            matrix_ref[rows, t * TILE : (t + 1) * TILE] = dense_block(t * tiles + u).T.astype(BF16)
            return carry

        lax.fori_loop(0, tiles, put, 0)
    loads[4].wait()
    eye = iota((TILE, TILE), 0) == iota((TILE, TILE), 1)
    for t in range(tiles):
        block = dense_block(t * tiles + t) + diag_ref[t].astype(F32)
        here_rows = slice(t * TILE, (t + 1) * TILE)
        level_ref[:, here_rows] = jnp.sum(jnp.where(eye, block, 0.0), axis=0, keepdims=True)
        matrix_ref[here_rows, here_rows] = jnp.where(eye, 0.0, block).T.astype(BF16)

    loads[5].wait()
    wide[...] = probe_ref[...].astype(F32)
    for t in range(tiles):
        basis_ref[:, t * TILE : (t + 1) * TILE] = wide[pl.ds(t, basis_ref.shape[0], stride=tiles), :]

    loads[6].wait()
    for copy in copies:
        copy.wait()
    zero = jnp.zeros(stiff_ref.shape, F32)
    stiff = stiff_ref[...]

    def face_value(face):
        dim, high = face // 2, face % 2
        inside = here[dim] < sizes[dim] - 1 if high else here[dim] > 0
        return jnp.where(inside, got[face], zero)

    total = face_value(1) + face_value(0)
    row = iota(stiff.shape, 0)
    y_low, y_high = face_value(2), face_value(3)
    total = total + jnp.where(row == 0, pltpu.roll(stiff, 1, 0), y_high[0:1, :])
    total = total + jnp.where(row == 1, pltpu.roll(stiff, 1, 0), y_low[1:2, :])
    lane = iota(stiff.shape, 1)
    z_low, z_high = face_value(4), face_value(5)
    width = stiff.shape[1]
    total = total + jnp.where(
        lane == width - 1, z_high[:, 0:1], pltpu.roll(stiff, width - 1, 1)
    )
    total = total + jnp.where(lane == 0, z_low[:, width - 1 : width], pltpu.roll(stiff, 1, 1))
    weight_ref[...] = stiff / (stiff + total / 6.0)


def in_hbm(x):
    return pltpu.with_memory_space_constraint(x, pltpu.HBM)


def sketch_operands(probes, stiff, diagonal, off_block, rows, cols, count):
    vmem = pl.BlockSpec(memory_space=pltpu.VMEM)
    hbm = pl.BlockSpec(memory_space=pltpu.HBM)
    dma = pltpu.SemaphoreType.DMA
    tiles, slots = diagonal.shape[0], off_block.shape[0]
    total = tiles * TILE
    return pl.pallas_call(
        operands_kernel,
        out_shape=(
            jax.ShapeDtypeStruct(stiff.shape, F32),
            jax.ShapeDtypeStruct((probes.shape[0] // tiles, total), F32),
            jax.ShapeDtypeStruct((1, total), F32),
            jax.ShapeDtypeStruct((total, total), BF16),
        ),
        in_specs=[hbm] * 7,
        out_specs=(vmem, vmem, vmem, vmem),
        scratch_shapes=[
            pltpu.VMEM((6,) + stiff.shape, F32),
            pltpu.VMEM(stiff.shape, F32),
            pltpu.SMEM(rows.shape, jnp.int32),
            pltpu.SMEM(cols.shape, jnp.int32),
            pltpu.SMEM(count.shape, jnp.int32),
            pltpu.SMEM(rows.shape, jnp.int32),
            pltpu.VMEM(probes.shape, BF16),
            pltpu.VMEM(diagonal.shape, BF16),
            pltpu.VMEM(off_block.shape, BF16),
            pltpu.VMEM(probes.shape, F32),
            pltpu.VMEM((slots + 1, TILE, TILE), F32),
            dma((6,)),
            dma((6,)),
            dma((7,)),
        ],
        compiler_params=pltpu.CompilerParams(
            collective_id=0, has_side_effects=True, vmem_limit_bytes=24 * 2**20
        ),
        name="sketch_operands",
    )(*map(in_hbm, (stiff, rows, cols)), count, *map(in_hbm, (probes, diagonal, off_block)))


def eliminate(gram):
    count = gram.shape[0]
    start = jnp.concatenate([gram, (iota(gram.shape, 0) == iota(gram.shape, 1)).astype(F32)], 1)
    row = iota((count, 1), 0)
    work = start
    pivots = jnp.zeros((count, 1), F32)
    for j in range(count):
        column = work[:, j : j + 1]
        pivot = column[j : j + 1, :]
        factor = jnp.where(row > j, column * (1.0 / pivot), 0.0)
        pivots = jnp.where(row == j, column, pivots)
        work = work - factor * work[j : j + 1, :]
    inverse = work[:, count:] * lax.rsqrt(pivots)
    original = jnp.sum(
        jnp.where(iota(gram.shape, 0) == iota(gram.shape, 1), gram, 0.0), axis=1, keepdims=True
    )
    return inverse, jnp.min(pivots / original)


def split(x):
    high = x.astype(BF16)
    return high, (x - high.astype(F32)).astype(BF16)


def basis_kernel(basis_ref, weight_ref, level_ref, matrix, defl_ref, field_ref, self_ref, wide):
    total = basis_ref.shape[1]
    tiles = total // TILE
    level = level_ref[...]
    weight = weight_ref[...]
    weight = jnp.concatenate([weight[0:1, :], weight[1:2, :]] * (tiles // 2), axis=1)
    step_weight = weight * (1.0 / SHIFT)

    def apply(high, low):
        both = jnp.dot(
            jnp.concatenate([high, low], axis=0), matrix[...], preferred_element_type=F32
        )
        return both[: high.shape[0]] + both[high.shape[0] :]

    def image_of(basis):
        scaled = basis * weight
        return basis - step_weight * (apply(*split(scaled)) + level * scaled)

    def normaliser(image):
        return eliminate(dot_nt(image, image, HIGHEST) * (1.0 / total))

    def finish(inverse, image):
        kept = jnp.dot(inverse, image, preferred_element_type=F32, precision=HIGHEST)[:DEFL]
        for t in range(tiles):
            wide[pl.ds(t, DEFL, stride=tiles), :] = kept[:, t * TILE : (t + 1) * TILE]
        defl_ref[...] = wide[...].astype(BF16)
        weighted = (kept * weight).astype(BF16)
        for t in range(tiles):
            field_ref[t % 2, :, t // 2 * TILE : (t // 2 + 1) * TILE] = weighted[
                :, t * TILE : (t + 1) * TILE
            ]
        applied = jnp.dot(weighted, matrix[...], preferred_element_type=F32)
        applied = applied + level * weighted.astype(F32)
        high, low = split(applied)
        self_ref[...] = (dot_nt(weighted, high) + dot_nt(weighted, low)) * (1.0 / total)

    image = basis_ref[...]
    for _ in range(ITERS):
        image = image_of(image)
    inverse, least = normaliser(image)
    finish(inverse, image)

    @pl.when(jnp.logical_not(least > SAFE_PIVOT))
    def _():
        def iteration(_, basis):
            image = image_of(basis)
            inverse, _ = normaliser(image)
            return jnp.dot(inverse, image, preferred_element_type=F32, precision=HIGHEST)

        basis = lax.fori_loop(0, ITERS - 1, iteration, basis_ref[...])
        image = image_of(basis)
        inverse, _ = normaliser(image)
        finish(inverse, image)


def local_basis(basis, weight, level, matrix):
    total = basis.shape[1]
    vmem = pl.BlockSpec(memory_space=pltpu.VMEM)
    return pl.pallas_call(
        basis_kernel,
        out_shape=(
            jax.ShapeDtypeStruct((DEFL * total // TILE, TILE), BF16),
            jax.ShapeDtypeStruct((2, DEFL, total // 2), BF16),
            jax.ShapeDtypeStruct((DEFL, DEFL), F32),
        ),
        in_specs=[vmem] * 4,
        out_specs=(vmem, vmem, vmem),
        scratch_shapes=[pltpu.VMEM((DEFL * total // TILE, TILE), F32)],
        compiler_params=pltpu.CompilerParams(vmem_limit_bytes=24 * 2**20),
        name="local_basis",
    )(basis, weight, level, matrix)


PLANE = 9
OWN = 4
PARTS = 16
PAYLOAD_ROWS = 16
ROW_GROUPS = 24
PAYLOAD_LANES = ROW_GROUPS * DEFL
BLOCK_GROUPS = PLANE * DEFL
END_GROUPS = 36


def plane_step(m):
    return m // 3 - 1, m % 3 - 1


def facing(m):
    return {-1: (1,), 0: (0, 1), 1: (0,)}[plane_step(m)[1]]


def end_group(m, y, c):
    before = sum(3 * len(facing(i)) for i in range(m))
    return before + 3 * facing(m).index(y) + c


def end_picker(y, half):
    row, lane = iota((PARTS, half), 0), iota((PARTS, half), 1)
    end, part = row // 8, row % 8
    hit = (part // 3 == y) & (part < 6) & (lane == (part % 3) * TILE + end * (TILE - 1))
    return hit.astype(BF16)


def payload_group(rows):
    group = DEFL + PARTS
    m, r = rows // group, rows % group
    first = jnp.zeros(rows.shape, jnp.int32)
    for i in range(1, PLANE):
        first = jnp.where(m == i, end_group(i, facing(i)[0], 0), first)
    low_y = jnp.where(m % 3 == 0, 1, 0)
    count = jnp.where(m % 3 == 1, 6, 3)
    end, part = (r - DEFL) // 8, (r - DEFL) % 8 - 3 * low_y
    used = (part >= 0) & (part < count)
    ends = jnp.where(used, BLOCK_GROUPS + end * END_GROUPS + first + part, -1)
    return jnp.where(r < DEFL, m * DEFL + r, ends)


def line_tree():
    side = [(0, 5), (0, 2), (2, 1), (2, 3), (5, 4), (5, 6), (5, 7)]
    return side + [(-a, -b) for a, b in side] + [(5, 8)]


def exchange_kernel(
    field_ref, self_ref, out_ref, full, sides, line_slots, send_sem, recv_sem, line_send, line_recv
):
    n_x, n_y, n_z = (lax.axis_size(a) for a in ("gx", "gy", "gz"))
    my_x, my_y, my_z = (lax.axis_index(a) for a in ("gx", "gy", "gz"))
    half = field_ref.shape[2]
    tree = line_tree()

    def device(m):
        step_x, step_y = plane_step(m)
        return (lax.rem(my_x + step_x + n_x, n_x), lax.rem(my_y + step_y + n_y, n_y), my_z)

    def line(step):
        return (my_x, my_y, lax.rem(my_z + step + n_z, n_z))

    neighbours = [m for m in range(PLANE) if m != OWN]
    distances = sorted({abs(b - a) for a, b in tree})
    barrier = pltpu.get_barrier_semaphore()
    for distance in reversed(distances):
        for step in (-distance, distance):
            pl.semaphore_signal(barrier, inc=1, device_id=line(step), device_id_type=MESH)
    for m in neighbours:
        pl.semaphore_signal(barrier, inc=1, device_id=device(m), device_id_type=MESH)
    pl.semaphore_wait(barrier, len(neighbours) + 2 * len(distances))

    slot = {m: i for i, m in enumerate(m for m in neighbours if plane_step(m)[1] != 0)}
    copies = []
    for m in neighbours:
        step_x, step_y = plane_step(m)
        back = PLANE - 1 - m
        if step_y == 0:
            source, target = field_ref, full.at[back // 3 // 2]
        else:
            source, target = field_ref.at[1 if step_y > 0 else 0], sides.at[slot[back]]
        copy = pltpu.make_async_remote_copy(
            src_ref=source,
            dst_ref=target,
            send_sem=send_sem.at[m],
            recv_sem=recv_sem.at[back],
            device_id=device(m),
            device_id_type=MESH,
        )
        copy.start()
        copies.append(copy)

    pick = [end_picker(y, half) for y in range(2)]
    own = [field_ref[y] for y in range(2)]
    stack = [[jnp.concatenate([-own[y], pick[z]], axis=0) for z in range(2)] for y in range(2)]
    lanes = PAYLOAD_LANES
    spread = (iota((DEFL, lanes), 1) % DEFL == iota((DEFL, lanes), 0)).astype(BF16)
    rows = PLANE * (DEFL + PARTS)
    place = payload_group(iota((rows, 1), 0)) % ROW_GROUPS
    keep = iota((rows, lanes), 1) // DEFL == place
    target = payload_group(iota((PAYLOAD_ROWS, rows), 1))
    gather = (target >= 0) & (target // ROW_GROUPS == iota((PAYLOAD_ROWS, rows), 0))
    gather = gather.astype(BF16)
    for copy in copies:
        copy.wait_recv()

    parts = []
    for m in range(PLANE):
        step_x, step_y = plane_step(m)
        if m == OWN:
            ends = dot_nt(pick[0], own[0]) + dot_nt(pick[1], own[1])
            parts.append(jnp.concatenate([self_ref[...], ends], axis=0))
            continue
        if step_y == 0:
            side = m // 3 // 2
            block = dot_nt(stack[0][0], full[side, 0]) + dot_nt(stack[1][1], full[side, 1])
        elif step_y < 0:
            block = dot_nt(stack[0][1], sides[slot[m]])
        else:
            block = dot_nt(stack[1][0], sides[slot[m]])
        inside = True
        if step_x != 0:
            inside = my_x < n_x - 1 if step_x > 0 else my_x > 0
        if step_y != 0:
            inside = jnp.logical_and(inside, my_y < n_y - 1 if step_y > 0 else my_y > 0)
        parts.append(jnp.where(inside, block, 0.0))
    parts = jnp.concatenate(parts, axis=0).astype(BF16)

    wide = jnp.dot(parts, spread, preferred_element_type=F32)
    wide = jnp.where(keep, wide, 0.0).astype(BF16)
    line_slots[my_z] = jnp.dot(gather, wide, preferred_element_type=F32).astype(BF16)

    sign = 1 - 2 * lax.rem(my_x, 2)
    hops = {}

    def send(parent, child):
        owner = line_slots.at[lax.rem(my_z - sign * parent + n_z, n_z)]
        hop = pltpu.make_async_remote_copy(
            src_ref=owner,
            dst_ref=owner,
            send_sem=line_send.at[child + n_z // 2],
            recv_sem=line_recv.at[child + n_z // 2],
            device_id=line(sign * (child - parent)),
            device_id_type=MESH,
        )
        hop.start()
        hops[child] = hop

    for parent, child in tree:
        if parent == 0:
            send(parent, child)
    parents = [p for p in sorted({p for p, _ in tree}, key=abs) if p != 0]
    for p in parents:
        hops[p].wait_recv()
        for parent, child in tree:
            if parent == p:
                send(parent, child)
    for child, hop in hops.items():
        if child not in parents:
            hop.wait_recv()
    for copy in copies + list(hops.values()):
        copy.wait_send()
    out_ref[...] = line_slots[...]


def exchange(field, self_block, n_z):
    vmem = pl.BlockSpec(memory_space=pltpu.VMEM)
    dma = pltpu.SemaphoreType.DMA
    half = field.shape[2]
    payload = (n_z, PAYLOAD_ROWS, PAYLOAD_LANES)
    return pl.pallas_call(
        exchange_kernel,
        out_shape=jax.ShapeDtypeStruct(payload, BF16),
        in_specs=[vmem, vmem],
        out_specs=vmem,
        scratch_shapes=[
            pltpu.VMEM((2, 2, DEFL, half), BF16),
            pltpu.VMEM((6, DEFL, half), BF16),
            pltpu.VMEM(payload, BF16),
            dma((PLANE,)),
            dma((PLANE,)),
            dma((n_z + 1,)),
            dma((n_z + 1,)),
        ],
        compiler_params=pltpu.CompilerParams(
            collective_id=1, has_side_effects=True, vmem_limit_bytes=24 * 2**20
        ),
        name="exchange",
    )(field, self_block)


def pair_index(m, step_z):
    flat = 3 * m + step_z + 1
    return flat if flat < 13 else flat - 1


def unpack_kernel(gathered_ref, self_ref, pairs_ref):
    n_z = self_ref.shape[0]
    width = DEFL * DEFL
    packed = gathered_ref[...]
    column = iota((1, n_z * PAYLOAD_ROWS), 1)

    def select(first, count, shift):
        index = iota((count * n_z, 1), 0)
        member = index % n_z + shift
        inside = (member >= 0) & (member < n_z)
        wanted = jnp.where(inside, member * PAYLOAD_ROWS + first + index // n_z, -1)
        hit = (column == wanted).astype(BF16)
        return jnp.dot(hit, packed, preferred_element_type=F32)

    block_rows = BLOCK_GROUPS // ROW_GROUPS
    rows = select(0, block_rows, 0)
    for m in range(PLANE):
        pieces, group = [], m * DEFL
        while group < (m + 1) * DEFL:
            row, start = group // ROW_GROUPS, group % ROW_GROUPS
            stop = min(ROW_GROUPS, start + (m + 1) * DEFL - group)
            pieces.append(rows[row * n_z : (row + 1) * n_z, start * DEFL : stop * DEFL])
            group += stop - start
        block = jnp.concatenate(pieces, axis=1)
        if m == OWN:
            self_ref[...] = block
        else:
            pairs_ref[pair_index(m, 0)] = block

    per_tile = TILE // DEFL
    row_tiles = ROW_GROUPS // per_tile
    end_tiles = END_GROUPS // per_tile
    end_rows = 2 * END_GROUPS // ROW_GROUPS

    def tile_of(rows, number):
        row, i = number // row_tiles, number % row_tiles
        return rows[row * n_z : (row + 1) * n_z, i * TILE : (i + 1) * TILE]

    own_first = end_group(OWN, 0, 0) // per_tile
    own_count = end_group(OWN, 1, 2) // per_tile + 1 - own_first
    rows = select(block_rows, end_rows, 0).astype(BF16)
    own_tiles = jnp.concatenate(
        [tile_of(rows, end * end_tiles + own_first + i) for end in range(2) for i in range(own_count)],
        axis=0,
    )
    value, lane = iota((TILE, width), 0), iota((TILE, width), 1)
    own = []
    for v in range(per_tile):
        spread = jnp.where(value == v * DEFL + lane // DEFL, -1.0, 0.0).astype(BF16)
        own.append(jnp.dot(own_tiles, spread, preferred_element_type=F32))

    def own_part(end, y, c):
        group = end_group(OWN, y, c)
        start = (end * own_count + group // per_tile - own_first) * n_z
        return own[group % per_tile][start : start + n_z]

    value, lane = iota((TILE, per_tile * TILE), 0), iota((TILE, per_tile * TILE), 1)
    repeat = (value == lane // TILE * DEFL + lane % DEFL).astype(BF16)
    for step_z in (-1, 1):
        their_end, own_end = (0, 1) if step_z > 0 else (1, 0)
        rows = select(block_rows, end_rows, step_z).astype(BF16)
        tiles = [tile_of(rows, their_end * end_tiles + i) for i in range(end_tiles)]
        theirs = jnp.dot(jnp.concatenate(tiles, axis=0), repeat, preferred_element_type=F32)
        for m in range(PLANE):
            step_y = plane_step(m)[1]
            pairs = [(0, 0), (1, 1)] if step_y == 0 else [(0, 1)] if step_y < 0 else [(1, 0)]
            total = None
            for own_y, their_y in pairs:
                for c in range(3):
                    group = end_group(m, their_y, c)
                    start, v = group // per_tile * n_z, group % per_tile
                    right = theirs[start : start + n_z, v * TILE : (v + 1) * TILE]
                    right = jnp.concatenate([right] * (width // TILE), axis=1)
                    term = own_part(own_end, own_y, c) * right
                    total = term if total is None else total + term
            pairs_ref[pair_index(m, step_z)] = total


def unpack(gathered, n_z):
    vmem = pl.BlockSpec(memory_space=pltpu.VMEM)
    width = DEFL * DEFL
    return pl.pallas_call(
        unpack_kernel,
        out_shape=(
            jax.ShapeDtypeStruct((n_z, width), F32),
            jax.ShapeDtypeStruct((26, n_z, width), F32),
        ),
        in_specs=[vmem],
        out_specs=(vmem, vmem),
        compiler_params=pltpu.CompilerParams(vmem_limit_bytes=32 * 2**20),
        name="unpack",
    )(gathered.reshape(n_z * PAYLOAD_ROWS, PAYLOAD_LANES))


def per_device(probes, stiffness, diag_tiles, off_tiles, off_rows, off_cols, off_count):
    n_z = lax.axis_size("gz")
    cell_shape = probes.shape[1:]
    weight, basis, level, matrix = sketch_operands(
        probes.reshape(-1, TILE),
        stiffness[0],
        diag_tiles[0, 0, 0],
        off_tiles[0, 0, 0],
        off_rows[0, 0, 0],
        off_cols[0, 0, 0],
        off_count[0, 0],
    )
    deflation, field, self_block = local_basis(basis, weight, level, matrix)
    gathered = exchange(field, self_block, n_z)
    coarse_self, coarse_pairs = unpack(gathered, n_z)
    return (
        deflation.reshape((DEFL,) + cell_shape),
        coarse_self[None, None],
        coarse_pairs.transpose(1, 0, 2)[None, None],
    )


def solution(mesh):
    placed = (
        P(None, None, "gx", "gy", "gz"),
        P("gx", "gy", "gz"),
        P("gx", "gy", "gz", None, None, None),
        P("gx", "gy", "gz", None, None, None),
        P("gx", "gy", "gz", None),
        P("gx", "gy", "gz", None),
        P("gx", "gy", "gz"),
    )
    return jax.shard_map(
        per_device,
        mesh=mesh,
        in_specs=placed,
        out_specs=(
            P(None, None, "gx", "gy", "gz"),
            P("gx", "gy", None, None),
            P("gx", "gy", None, None, None),
        ),
        check_vma=False,
    )
```

```python
import jax
import jax.numpy as jnp
from jax import lax
from jax.experimental import pallas as pl
from jax.experimental.pallas import tpu as pltpu
from jax.sharding import PartitionSpec as P

MESH = pl.DeviceIdType.MESH
F32 = jnp.float32
BF16 = jnp.bfloat16
HIGHEST = lax.Precision.HIGHEST

DEFL = 32
ITERS = 12
SHIFT = 8.0
TILE = 128
SAFE_PIVOT = 0.01
PANEL = 8


def iota(shape, dim):
    return lax.broadcasted_iota(jnp.int32, shape, dim)


def dot_nt(a, b, precision=None):
    return lax.dot_general(
        a, b, (((1,), (1,)), ((), ())), preferred_element_type=F32, precision=precision
    )


def operands_kernel(
    stiff_hbm, rows_hbm, cols_hbm, count_hbm, probe_hbm, diag_hbm, off_hbm,
    weight_ref, basis_ref, level_ref, matrix_ref,
    got, stiff_ref, rows_ref, cols_ref, count_ref, key_ref, probe_ref, diag_ref, off_ref, wide, sums,
    send_sem, recv_sem, local_sem,
):
    sizes = [lax.axis_size(a) for a in ("gx", "gy", "gz")]
    here = [lax.axis_index(a) for a in ("gx", "gy", "gz")]
    slots, tiles = off_ref.shape[0], diag_ref.shape[0]
    faces = []
    for dim, size in enumerate(sizes):
        for step in (-1, 1):
            there = list(here)
            there[dim] = lax.rem(here[dim] + step + size, size)
            faces.append(tuple(there))
    barrier = pltpu.get_barrier_semaphore()
    for there in faces:
        pl.semaphore_signal(barrier, inc=1, device_id=there, device_id_type=MESH)
    loads = []
    for source, target in (
        (rows_hbm, rows_ref),
        (cols_hbm, cols_ref),
        (count_hbm, count_ref),
        (off_hbm, off_ref),
        (diag_hbm, diag_ref),
        (probe_hbm, probe_ref),
        (stiff_hbm, stiff_ref),
    ):
        load = pltpu.make_async_copy(source, target, local_sem.at[len(loads)])
        load.start()
        loads.append(load)
    pl.semaphore_wait(barrier, len(faces))
    copies = []
    for face, there in enumerate(faces):
        copy = pltpu.make_async_remote_copy(
            src_ref=stiff_hbm,
            dst_ref=got.at[face ^ 1],
            send_sem=send_sem.at[face],
            recv_sem=recv_sem.at[face ^ 1],
            device_id=there,
            device_id_type=MESH,
        )
        copy.start()
        copies.append(copy)

    for load in loads[:3]:
        load.wait()
    count = count_ref[0]
    for m in range(slots):
        key_ref[m] = jnp.where(m < count, rows_ref[m] * tiles + cols_ref[m], -1 - m)
    sums[slots] = jnp.zeros((TILE, TILE), F32)
    loads[3].wait()

    def add_tile(m, carry):
        key, before = key_ref[m], slots
        for other in range(slots - 1):
            before = jnp.where((other < m) & (key_ref[other] == key), other, before)
        sums[m] = off_ref[m].astype(F32) + sums[before]
        return carry

    lax.fori_loop(0, slots, add_tile, 0)

    def dense_block(place):
        last = slots
        for m in range(slots):
            last = jnp.where(key_ref[m] == place, m, last)
        return sums[last]

    loads[4].wait()
    eye = iota((TILE, TILE), 0) == iota((TILE, TILE), 1)
    for t in range(tiles):
        columns = slice(t * TILE, (t + 1) * TILE)
        for u in range(tiles):
            block = dense_block(t * tiles + u)
            if t == u:
                block = block + diag_ref[t].astype(F32)
                level_ref[:, columns] = jnp.sum(jnp.where(eye, block, 0.0), axis=0, keepdims=True)
                block = jnp.where(eye, 0.0, block)
            matrix_ref[u * TILE : (u + 1) * TILE, columns] = block.astype(BF16).T

    loads[5].wait()
    wide[...] = probe_ref[...].astype(F32)
    for t in range(tiles):
        basis_ref[:, t * TILE : (t + 1) * TILE] = wide[pl.ds(t, basis_ref.shape[0], stride=tiles), :]

    loads[6].wait()
    for copy in copies:
        copy.wait()
    zero = jnp.zeros(stiff_ref.shape, F32)
    stiff = stiff_ref[...]

    def face_value(face):
        dim, high = face // 2, face % 2
        inside = here[dim] < sizes[dim] - 1 if high else here[dim] > 0
        return jnp.where(inside, got[face], zero)

    total = face_value(1) + face_value(0)
    row = iota(stiff.shape, 0)
    y_low, y_high = face_value(2), face_value(3)
    total = total + jnp.where(row == 0, pltpu.roll(stiff, 1, 0), y_high[0:1, :])
    total = total + jnp.where(row == 1, pltpu.roll(stiff, 1, 0), y_low[1:2, :])
    lane = iota(stiff.shape, 1)
    z_low, z_high = face_value(4), face_value(5)
    width = stiff.shape[1]
    total = total + jnp.where(
        lane == width - 1, z_high[:, 0:1], pltpu.roll(stiff, width - 1, 1)
    )
    total = total + jnp.where(lane == 0, z_low[:, width - 1 : width], pltpu.roll(stiff, 1, 1))
    weight_ref[...] = stiff / (stiff + total / 6.0)


def in_hbm(x):
    return pltpu.with_memory_space_constraint(x, pltpu.HBM)


def sketch_operands(probes, stiff, diagonal, off_block, rows, cols, count):
    vmem = pl.BlockSpec(memory_space=pltpu.VMEM)
    hbm = pl.BlockSpec(memory_space=pltpu.HBM)
    dma = pltpu.SemaphoreType.DMA
    tiles, slots = diagonal.shape[0], off_block.shape[0]
    total = tiles * TILE
    return pl.pallas_call(
        operands_kernel,
        out_shape=(
            jax.ShapeDtypeStruct(stiff.shape, F32),
            jax.ShapeDtypeStruct((probes.shape[0] // tiles, total), F32),
            jax.ShapeDtypeStruct((1, total), F32),
            jax.ShapeDtypeStruct((total, total), BF16),
        ),
        in_specs=[hbm] * 7,
        out_specs=(vmem, vmem, vmem, vmem),
        scratch_shapes=[
            pltpu.VMEM((6,) + stiff.shape, F32),
            pltpu.VMEM(stiff.shape, F32),
            pltpu.SMEM(rows.shape, jnp.int32),
            pltpu.SMEM(cols.shape, jnp.int32),
            pltpu.SMEM(count.shape, jnp.int32),
            pltpu.SMEM(rows.shape, jnp.int32),
            pltpu.VMEM(probes.shape, BF16),
            pltpu.VMEM(diagonal.shape, BF16),
            pltpu.VMEM(off_block.shape, BF16),
            pltpu.VMEM(probes.shape, F32),
            pltpu.VMEM((slots + 1, TILE, TILE), F32),
            dma((6,)),
            dma((6,)),
            dma((7,)),
        ],
        compiler_params=pltpu.CompilerParams(
            collective_id=0, has_side_effects=True, vmem_limit_bytes=24 * 2**20
        ),
        name="sketch_operands",
    )(*map(in_hbm, (stiff, rows, cols)), count, *map(in_hbm, (probes, diagonal, off_block)))


def eliminate(gram):
    count = gram.shape[0]
    start = jnp.concatenate([gram, (iota(gram.shape, 0) == iota(gram.shape, 1)).astype(F32)], 1)
    rows_done, pivots_done = [], []
    work = start
    for first in range(0, count, PANEL):
        row = iota((count - first, 1), 0)
        columns = [
            jnp.broadcast_to(work[:, j : j + 1], work.shape) for j in range(first, first + PANEL)
        ]
        for i in range(PANEL):
            factor = jnp.where(row > i, columns[i] * (1.0 / columns[i][i : i + 1, :]), 0.0)
            pivots_done.append(columns[i][i : i + 1, :count])
            for k in range(i + 1, PANEL):
                columns[k] = columns[k] - factor * columns[k][i : i + 1, :]
            work = work - factor * work[i : i + 1, :]
        rows_done.append(work[:PANEL])
        work = work[PANEL:]
    work = jnp.concatenate(rows_done, axis=0)
    pivots = jnp.concatenate(pivots_done, axis=0)[:, :1]
    inverse = work[:, count:] * lax.rsqrt(pivots)
    original = jnp.sum(
        jnp.where(iota(gram.shape, 0) == iota(gram.shape, 1), gram, 0.0), axis=1, keepdims=True
    )
    return inverse, jnp.min(pivots / original)


def split(x):
    high = x.astype(BF16)
    return high, (x - high.astype(F32)).astype(BF16)


def unknown_weights(weight, tiles):
    return jnp.concatenate([weight[0:1, :], weight[1:2, :]] * (tiles // 2), axis=1)


def image_kernel(basis_ref, weight_ref, level_ref, matrix, inverse_ref, image_ref):
    total = basis_ref.shape[1]
    level = level_ref[...]
    weight = unknown_weights(weight_ref[...], total // TILE)
    step_weight = weight * (1.0 / SHIFT)

    def image_of(basis):
        scaled = basis * weight
        high, low = split(scaled)
        both = jnp.dot(
            jnp.concatenate([high, low], axis=0), matrix[...], preferred_element_type=F32
        )
        applied = both[: high.shape[0]] + both[high.shape[0] :] + level * scaled
        return basis - step_weight * applied

    def normaliser(image):
        return eliminate(dot_nt(image, image, HIGHEST) * (1.0 / total))

    image = basis_ref[...]
    for _ in range(ITERS):
        image = image_of(image)
    inverse, least = normaliser(image)
    inverse_ref[...] = inverse
    image_ref[...] = image

    @pl.when(jnp.logical_not(least > SAFE_PIVOT))
    def _():
        def iteration(_, basis):
            image = image_of(basis)
            inverse, _ = normaliser(image)
            return jnp.dot(inverse, image, preferred_element_type=F32, precision=HIGHEST)

        basis = lax.fori_loop(0, ITERS - 1, iteration, basis_ref[...])
        image = image_of(basis)
        inverse, _ = normaliser(image)
        inverse_ref[...] = inverse
        image_ref[...] = image


def last_image(basis, weight, level, matrix):
    probes = basis.shape[0]
    vmem = pl.BlockSpec(memory_space=pltpu.VMEM)
    return pl.pallas_call(
        image_kernel,
        out_shape=(
            jax.ShapeDtypeStruct((probes, probes), F32),
            jax.ShapeDtypeStruct(basis.shape, F32),
        ),
        in_specs=[vmem] * 4,
        out_specs=(vmem, vmem),
        compiler_params=pltpu.CompilerParams(vmem_limit_bytes=24 * 2**20),
        name="last_image",
    )(basis, weight, level, matrix)


PLANE = 9
OWN = 4
PARTS = 16
PAYLOAD_ROWS = 16
ROW_GROUPS = 24
PAYLOAD_LANES = ROW_GROUPS * DEFL
BLOCK_GROUPS = PLANE * DEFL
END_GROUPS = 36


def plane_step(m):
    return m // 3 - 1, m % 3 - 1


def facing(m):
    return {-1: (1,), 0: (0, 1), 1: (0,)}[plane_step(m)[1]]


def end_group(m, y, c):
    before = sum(3 * len(facing(i)) for i in range(m))
    return before + 3 * facing(m).index(y) + c


def end_picker(y, half):
    row, lane = iota((PARTS, half), 0), iota((PARTS, half), 1)
    end, part = row // 8, row % 8
    hit = (part // 3 == y) & (part < 6) & (lane == (part % 3) * TILE + end * (TILE - 1))
    return hit.astype(BF16)


def payload_group(rows):
    group = DEFL + PARTS
    m, r = rows // group, rows % group
    first = jnp.zeros(rows.shape, jnp.int32)
    for i in range(1, PLANE):
        first = jnp.where(m == i, end_group(i, facing(i)[0], 0), first)
    low_y = jnp.where(m % 3 == 0, 1, 0)
    count = jnp.where(m % 3 == 1, 6, 3)
    end, part = (r - DEFL) // 8, (r - DEFL) % 8 - 3 * low_y
    used = (part >= 0) & (part < count)
    ends = jnp.where(used, BLOCK_GROUPS + end * END_GROUPS + first + part, -1)
    return jnp.where(r < DEFL, m * DEFL + r, ends)


def line_tree():
    side = [(0, 5), (0, 2), (2, 1), (2, 3), (5, 4), (5, 6), (5, 7)]
    return side + [(-a, -b) for a, b in side] + [(5, 8)]


def exchange_kernel(
    inverse_ref, image_ref, weight_ref, level_ref, matrix_ref,
    out_ref, defl_ref,
    field_ref, full, sides, line_slots, wide_ref, send_sem, recv_sem, line_send, line_recv,
):
    n_x, n_y, n_z = (lax.axis_size(a) for a in ("gx", "gy", "gz"))
    my_x, my_y, my_z = (lax.axis_index(a) for a in ("gx", "gy", "gz"))
    half = field_ref.shape[2]
    tree = line_tree()

    def device(m):
        step_x, step_y = plane_step(m)
        return (lax.rem(my_x + step_x + n_x, n_x), lax.rem(my_y + step_y + n_y, n_y), my_z)

    def line(step):
        return (my_x, my_y, lax.rem(my_z + step + n_z, n_z))

    neighbours = [m for m in range(PLANE) if m != OWN]
    distances = sorted({abs(b - a) for a, b in tree})
    barrier = pltpu.get_barrier_semaphore()
    for distance in reversed(distances):
        for step in (-distance, distance):
            pl.semaphore_signal(barrier, inc=1, device_id=line(step), device_id_type=MESH)
    for m in neighbours:
        pl.semaphore_signal(barrier, inc=1, device_id=device(m), device_id_type=MESH)

    total = image_ref.shape[1]
    tiles = total // TILE
    basis = jnp.dot(
        inverse_ref[...], image_ref[...], preferred_element_type=F32, precision=HIGHEST
    )
    kept = basis[:DEFL]
    weighted = (kept * unknown_weights(weight_ref[...], tiles)).astype(BF16)
    for t in range(tiles):
        field_ref[t % 2, :, t // 2 * TILE : (t // 2 + 1) * TILE] = weighted[
            :, t * TILE : (t + 1) * TILE
        ]
    pl.semaphore_wait(barrier, len(neighbours) + 2 * len(distances))

    slot = {m: i for i, m in enumerate(m for m in neighbours if plane_step(m)[1] != 0)}
    copies = []
    for m in neighbours:
        step_x, step_y = plane_step(m)
        back = PLANE - 1 - m
        if step_y == 0:
            source, target = field_ref, full.at[back // 3 // 2]
        else:
            source, target = field_ref.at[1 if step_y > 0 else 0], sides.at[slot[back]]
        copy = pltpu.make_async_remote_copy(
            src_ref=source,
            dst_ref=target,
            send_sem=send_sem.at[m],
            recv_sem=recv_sem.at[back],
            device_id=device(m),
            device_id_type=MESH,
        )
        copy.start()
        copies.append(copy)

    for t in range(tiles):
        wide_ref[pl.ds(t, DEFL, stride=tiles), :] = kept[:, t * TILE : (t + 1) * TILE]
    defl_ref[...] = wide_ref[...].astype(BF16)
    applied = jnp.dot(weighted, matrix_ref[...], preferred_element_type=F32)
    applied = applied + level_ref[...] * weighted.astype(F32)
    high, low = split(applied)
    self_block = (dot_nt(weighted, high) + dot_nt(weighted, low)) * (1.0 / total)

    pick = [end_picker(y, half) for y in range(2)]
    own = [field_ref[y] for y in range(2)]
    stack = [[jnp.concatenate([-own[y], pick[z]], axis=0) for z in range(2)] for y in range(2)]
    lanes = PAYLOAD_LANES
    spread = (iota((DEFL, lanes), 1) % DEFL == iota((DEFL, lanes), 0)).astype(BF16)
    rows = PLANE * (DEFL + PARTS)
    place = payload_group(iota((rows, 1), 0)) % ROW_GROUPS
    keep = iota((rows, lanes), 1) // DEFL == place
    target = payload_group(iota((PAYLOAD_ROWS, rows), 1))
    gather = (target >= 0) & (target // ROW_GROUPS == iota((PAYLOAD_ROWS, rows), 0))
    gather = gather.astype(BF16)
    for copy in copies:
        copy.wait_recv()

    parts = []
    for m in range(PLANE):
        step_x, step_y = plane_step(m)
        if m == OWN:
            ends = dot_nt(pick[0], own[0]) + dot_nt(pick[1], own[1])
            parts.append(jnp.concatenate([self_block, ends], axis=0))
            continue
        if step_y == 0:
            side = m // 3 // 2
            block = dot_nt(stack[0][0], full[side, 0]) + dot_nt(stack[1][1], full[side, 1])
        elif step_y < 0:
            block = dot_nt(stack[0][1], sides[slot[m]])
        else:
            block = dot_nt(stack[1][0], sides[slot[m]])
        inside = True
        if step_x != 0:
            inside = my_x < n_x - 1 if step_x > 0 else my_x > 0
        if step_y != 0:
            inside = jnp.logical_and(inside, my_y < n_y - 1 if step_y > 0 else my_y > 0)
        parts.append(jnp.where(inside, block, 0.0))
    parts = jnp.concatenate(parts, axis=0).astype(BF16)

    wide = jnp.dot(parts, spread, preferred_element_type=F32)
    wide = jnp.where(keep, wide, 0.0).astype(BF16)
    line_slots[my_z] = jnp.dot(gather, wide, preferred_element_type=F32).astype(BF16)

    sign = 1 - 2 * lax.rem(my_x, 2)
    hops = {}

    def send(parent, child):
        owner = line_slots.at[lax.rem(my_z - sign * parent + n_z, n_z)]
        hop = pltpu.make_async_remote_copy(
            src_ref=owner,
            dst_ref=owner,
            send_sem=line_send.at[child + n_z // 2],
            recv_sem=line_recv.at[child + n_z // 2],
            device_id=line(sign * (child - parent)),
            device_id_type=MESH,
        )
        hop.start()
        hops[child] = hop

    for parent, child in tree:
        if parent == 0:
            send(parent, child)
    parents = [p for p in sorted({p for p, _ in tree}, key=abs) if p != 0]
    for p in parents:
        hops[p].wait_recv()
        for parent, child in tree:
            if parent == p:
                send(parent, child)
    for child, hop in hops.items():
        if child not in parents:
            hop.wait_recv()
    for copy in copies + list(hops.values()):
        copy.wait_send()
    out_ref[...] = line_slots[...]


def exchange(inverse, image, weight, level, matrix, n_z):
    vmem = pl.BlockSpec(memory_space=pltpu.VMEM)
    dma = pltpu.SemaphoreType.DMA
    total = image.shape[1]
    payload = (n_z, PAYLOAD_ROWS, PAYLOAD_LANES)
    rows = DEFL * total // TILE
    return pl.pallas_call(
        exchange_kernel,
        out_shape=(
            jax.ShapeDtypeStruct(payload, BF16),
            jax.ShapeDtypeStruct((rows, TILE), BF16),
        ),
        in_specs=[vmem] * 5,
        out_specs=(vmem, vmem),
        scratch_shapes=[
            pltpu.VMEM((2, DEFL, total // 2), BF16),
            pltpu.VMEM((2, 2, DEFL, total // 2), BF16),
            pltpu.VMEM((6, DEFL, total // 2), BF16),
            pltpu.VMEM(payload, BF16),
            pltpu.VMEM((rows, TILE), F32),
            dma((PLANE,)),
            dma((PLANE,)),
            dma((n_z + 1,)),
            dma((n_z + 1,)),
        ],
        compiler_params=pltpu.CompilerParams(
            collective_id=1, has_side_effects=True, vmem_limit_bytes=24 * 2**20
        ),
        name="exchange",
    )(inverse, image, weight, level, matrix)


def pair_index(m, step_z):
    flat = 3 * m + step_z + 1
    return flat if flat < 13 else flat - 1


def unpack_kernel(
    gathered_ref, kept_ref, self_hbm, pairs_hbm, defl_hbm, self_ref, pairs_ref, sem
):
    n_z = self_ref.shape[0]
    width = DEFL * DEFL
    stores = []

    def store(source, target):
        copy = pltpu.make_async_copy(source, target, sem.at[len(stores)])
        copy.start()
        stores.append(copy)

    def store_pair(index, block):
        pairs_ref[index] = block
        store(pairs_ref.at[index], pairs_hbm.at[index])

    store(kept_ref, defl_hbm)
    packed = gathered_ref[...]
    column = iota((1, n_z * PAYLOAD_ROWS), 1)

    def select(first, count, shift):
        index = iota((count * n_z, 1), 0)
        member = index % n_z + shift
        inside = (member >= 0) & (member < n_z)
        wanted = jnp.where(inside, member * PAYLOAD_ROWS + first + index // n_z, -1)
        hit = (column == wanted).astype(BF16)
        return jnp.dot(hit, packed, preferred_element_type=F32)

    block_rows = BLOCK_GROUPS // ROW_GROUPS
    rows = select(0, block_rows, 0)
    for m in range(PLANE):
        pieces, group = [], m * DEFL
        while group < (m + 1) * DEFL:
            row, start = group // ROW_GROUPS, group % ROW_GROUPS
            stop = min(ROW_GROUPS, start + (m + 1) * DEFL - group)
            pieces.append(rows[row * n_z : (row + 1) * n_z, start * DEFL : stop * DEFL])
            group += stop - start
        block = jnp.concatenate(pieces, axis=1)
        if m == OWN:
            self_ref[...] = block
            store(self_ref, self_hbm)
        else:
            store_pair(pair_index(m, 0), block)

    per_tile = TILE // DEFL
    row_tiles = ROW_GROUPS // per_tile
    end_tiles = END_GROUPS // per_tile
    end_rows = 2 * END_GROUPS // ROW_GROUPS

    def tile_of(rows, number):
        row, i = number // row_tiles, number % row_tiles
        return rows[row * n_z : (row + 1) * n_z, i * TILE : (i + 1) * TILE]

    own_first = end_group(OWN, 0, 0) // per_tile
    own_count = end_group(OWN, 1, 2) // per_tile + 1 - own_first
    rows = select(block_rows, end_rows, 0).astype(BF16)
    own_tiles = jnp.concatenate(
        [tile_of(rows, end * end_tiles + own_first + i) for end in range(2) for i in range(own_count)],
        axis=0,
    )
    value, lane = iota((TILE, width), 0), iota((TILE, width), 1)
    own = []
    for v in range(per_tile):
        spread = jnp.where(value == v * DEFL + lane // DEFL, -1.0, 0.0).astype(BF16)
        own.append(jnp.dot(own_tiles, spread, preferred_element_type=F32))

    def own_part(end, y, c):
        group = end_group(OWN, y, c)
        start = (end * own_count + group // per_tile - own_first) * n_z
        return own[group % per_tile][start : start + n_z]

    value, lane = iota((TILE, per_tile * TILE), 0), iota((TILE, per_tile * TILE), 1)
    repeat = (value == lane // TILE * DEFL + lane % DEFL).astype(BF16)
    for step_z in (-1, 1):
        their_end, own_end = (0, 1) if step_z > 0 else (1, 0)
        rows = select(block_rows, end_rows, step_z).astype(BF16)
        tiles = [tile_of(rows, their_end * end_tiles + i) for i in range(end_tiles)]
        theirs = jnp.dot(jnp.concatenate(tiles, axis=0), repeat, preferred_element_type=F32)
        for m in range(PLANE):
            step_y = plane_step(m)[1]
            pairs = [(0, 0), (1, 1)] if step_y == 0 else [(0, 1)] if step_y < 0 else [(1, 0)]
            total = None
            for own_y, their_y in pairs:
                for c in range(3):
                    group = end_group(m, their_y, c)
                    start, v = group // per_tile * n_z, group % per_tile
                    right = theirs[start : start + n_z, v * TILE : (v + 1) * TILE]
                    right = jnp.concatenate([right] * (width // TILE), axis=1)
                    term = own_part(own_end, own_y, c) * right
                    total = term if total is None else total + term
            store_pair(pair_index(m, step_z), total)
    for copy in stores:
        copy.wait()


def unpack(gathered, kept, n_z):
    vmem = pl.BlockSpec(memory_space=pltpu.VMEM)
    hbm = pl.BlockSpec(memory_space=pltpu.HBM)
    width = DEFL * DEFL
    pairs = 3 * PLANE - 1
    return pl.pallas_call(
        unpack_kernel,
        out_shape=(
            jax.ShapeDtypeStruct((n_z, width), F32),
            jax.ShapeDtypeStruct((pairs, n_z, width), F32),
            jax.ShapeDtypeStruct(kept.shape, kept.dtype),
        ),
        in_specs=[vmem, vmem],
        out_specs=(hbm, hbm, hbm),
        scratch_shapes=[
            pltpu.VMEM((n_z, width), F32),
            pltpu.VMEM((pairs, n_z, width), F32),
            pltpu.SemaphoreType.DMA((pairs + 2,)),
        ],
        compiler_params=pltpu.CompilerParams(vmem_limit_bytes=32 * 2**20),
        name="unpack",
    )(gathered.reshape(n_z * PAYLOAD_ROWS, PAYLOAD_LANES), kept)


def per_device(probes, stiffness, diag_tiles, off_tiles, off_rows, off_cols, off_count):
    n_z = lax.axis_size("gz")
    cell_shape = probes.shape[1:]
    weight, basis, level, matrix = sketch_operands(
        probes.reshape(-1, TILE),
        stiffness[0],
        diag_tiles[0, 0, 0],
        off_tiles[0, 0, 0],
        off_rows[0, 0, 0],
        off_cols[0, 0, 0],
        off_count[0, 0],
    )
    inverse, image = last_image(basis, weight, level, matrix)
    gathered, kept = exchange(inverse, image, weight, level, matrix, n_z)
    coarse_self, coarse_pairs, deflation = unpack(gathered, kept, n_z)
    return (
        deflation.reshape((DEFL,) + cell_shape),
        coarse_self[None, None],
        coarse_pairs.transpose(1, 0, 2)[None, None],
    )


def solution(mesh):
    placed = (
        P(None, None, "gx", "gy", "gz"),
        P("gx", "gy", "gz"),
        P("gx", "gy", "gz", None, None, None),
        P("gx", "gy", "gz", None, None, None),
        P("gx", "gy", "gz", None),
        P("gx", "gy", "gz", None),
        P("gx", "gy", "gz"),
    )
    return jax.shard_map(
        per_device,
        mesh=mesh,
        in_specs=placed,
        out_specs=(
            P(None, None, "gx", "gy", "gz"),
            P("gx", "gy", None, None),
            P("gx", "gy", None, None, None),
        ),
        check_vma=False,
    )
```

```python
import functools

import jax
import jax.numpy as jnp
from jax import lax
from jax.experimental import pallas as pl
from jax.experimental.pallas import tpu as pltpu
from jax.sharding import PartitionSpec as P

MESH = pl.DeviceIdType.MESH
F32 = jnp.float32
BF16 = jnp.bfloat16
HIGHEST = lax.Precision.HIGHEST

DEFL = 32
ITERS = 12
SHIFT = 8.0
TILE = 128
SAFE_PIVOT = 0.01
PANEL = 8


def iota(shape, dim):
    return lax.broadcasted_iota(jnp.int32, shape, dim)


def over(x, n):
    return x >> (n.bit_length() - 1) if n & (n - 1) == 0 else x // n


def modulo(x, n):
    return x & (n - 1) if n & (n - 1) == 0 else x % n


def dot_nt(a, b, precision=None):
    return lax.dot_general(
        a, b, (((1,), (1,)), ((), ())), preferred_element_type=F32, precision=precision
    )


def operands_kernel(
    stiff_hbm, rows_hbm, cols_hbm, count_hbm, probe_hbm, diag_hbm, off_hbm,
    weight_ref, basis_ref, level_ref, matrix_ref,
    got, stiff_ref, rows_ref, cols_ref, count_ref, key_ref, probe_ref, diag_ref, off_ref, wide, sums,
    send_sem, recv_sem, local_sem,
):
    sizes = [lax.axis_size(a) for a in ("gx", "gy", "gz")]
    here = [lax.axis_index(a) for a in ("gx", "gy", "gz")]
    slots, tiles = off_ref.shape[0], diag_ref.shape[0]
    faces = []
    for dim, size in enumerate(sizes):
        for step in (-1, 1):
            there = list(here)
            there[dim] = lax.rem(here[dim] + step + size, size)
            faces.append(tuple(there))
    barrier = pltpu.get_barrier_semaphore()
    for there in faces:
        pl.semaphore_signal(barrier, inc=1, device_id=there, device_id_type=MESH)
    loads = []
    for source, target in (
        (rows_hbm, rows_ref),
        (cols_hbm, cols_ref),
        (count_hbm, count_ref),
        (off_hbm, off_ref),
        (diag_hbm, diag_ref),
        (probe_hbm, probe_ref),
        (stiff_hbm, stiff_ref),
    ):
        load = pltpu.make_async_copy(source, target, local_sem.at[len(loads)])
        load.start()
        loads.append(load)
    pl.semaphore_wait(barrier, len(faces))
    copies = []
    for face, there in enumerate(faces):
        copy = pltpu.make_async_remote_copy(
            src_ref=stiff_hbm,
            dst_ref=got.at[face ^ 1],
            send_sem=send_sem.at[face],
            recv_sem=recv_sem.at[face ^ 1],
            device_id=there,
            device_id_type=MESH,
        )
        copy.start()
        copies.append(copy)

    for load in loads[:3]:
        load.wait()
    count = count_ref[0]
    for m in range(slots):
        key_ref[m] = jnp.where(m < count, rows_ref[m] * tiles + cols_ref[m], -1 - m)
    sums[slots] = jnp.zeros((TILE, TILE), F32)
    loads[3].wait()

    def add_tile(m, carry):
        key, before = key_ref[m], slots
        for other in range(slots - 1):
            before = jnp.where((other < m) & (key_ref[other] == key), other, before)
        sums[m] = off_ref[m].astype(F32) + sums[before]
        return carry

    lax.fori_loop(0, slots, add_tile, 0)

    def dense_block(place):
        last = slots
        for m in range(slots):
            last = jnp.where(key_ref[m] == place, m, last)
        return sums[last]

    loads[4].wait()
    eye = iota((TILE, TILE), 0) == iota((TILE, TILE), 1)
    for t in range(tiles):
        columns = slice(t * TILE, (t + 1) * TILE)
        for u in range(tiles):
            block = dense_block(t * tiles + u)
            if t == u:
                block = block + diag_ref[t].astype(F32)
                level_ref[:, columns] = jnp.sum(jnp.where(eye, block, 0.0), axis=0, keepdims=True)
                block = jnp.where(eye, 0.0, block)
            matrix_ref[u * TILE : (u + 1) * TILE, columns] = block.astype(BF16).T

    loads[5].wait()
    wide[...] = probe_ref[...].astype(F32)
    for t in range(tiles):
        basis_ref[:, t * TILE : (t + 1) * TILE] = wide[pl.ds(t, basis_ref.shape[0], stride=tiles), :]

    loads[6].wait()
    for copy in copies:
        copy.wait()
    zero = jnp.zeros(stiff_ref.shape, F32)
    stiff = stiff_ref[...]

    def face_value(face):
        dim, high = face // 2, face % 2
        inside = here[dim] < sizes[dim] - 1 if high else here[dim] > 0
        return jnp.where(inside, got[face], zero)

    total = face_value(1) + face_value(0)
    row = iota(stiff.shape, 0)
    y_low, y_high = face_value(2), face_value(3)
    total = total + jnp.where(row == 0, pltpu.roll(stiff, 1, 0), y_high[0:1, :])
    total = total + jnp.where(row == 1, pltpu.roll(stiff, 1, 0), y_low[1:2, :])
    lane = iota(stiff.shape, 1)
    z_low, z_high = face_value(4), face_value(5)
    width = stiff.shape[1]
    total = total + jnp.where(
        lane == width - 1, z_high[:, 0:1], pltpu.roll(stiff, width - 1, 1)
    )
    total = total + jnp.where(lane == 0, z_low[:, width - 1 : width], pltpu.roll(stiff, 1, 1))
    weight_ref[...] = stiff / (stiff + total / 6.0)


def in_hbm(x):
    return pltpu.with_memory_space_constraint(x, pltpu.HBM)


def sketch_operands(probes, stiff, diagonal, off_block, rows, cols, count):
    vmem = pl.BlockSpec(memory_space=pltpu.VMEM)
    hbm = pl.BlockSpec(memory_space=pltpu.HBM)
    dma = pltpu.SemaphoreType.DMA
    tiles, slots = diagonal.shape[0], off_block.shape[0]
    total = tiles * TILE
    return pl.pallas_call(
        operands_kernel,
        out_shape=(
            jax.ShapeDtypeStruct(stiff.shape, F32),
            jax.ShapeDtypeStruct((probes.shape[0] // tiles, total), F32),
            jax.ShapeDtypeStruct((1, total), F32),
            jax.ShapeDtypeStruct((total, total), BF16),
        ),
        in_specs=[hbm] * 7,
        out_specs=(vmem, vmem, vmem, vmem),
        scratch_shapes=[
            pltpu.VMEM((6,) + stiff.shape, F32),
            pltpu.VMEM(stiff.shape, F32),
            pltpu.SMEM(rows.shape, jnp.int32),
            pltpu.SMEM(cols.shape, jnp.int32),
            pltpu.SMEM(count.shape, jnp.int32),
            pltpu.SMEM(rows.shape, jnp.int32),
            pltpu.VMEM(probes.shape, BF16),
            pltpu.VMEM(diagonal.shape, BF16),
            pltpu.VMEM(off_block.shape, BF16),
            pltpu.VMEM(probes.shape, F32),
            pltpu.VMEM((slots + 1, TILE, TILE), F32),
            dma((6,)),
            dma((6,)),
            dma((7,)),
        ],
        compiler_params=pltpu.CompilerParams(
            collective_id=0, has_side_effects=True, vmem_limit_bytes=24 * 2**20
        ),
        name="sketch_operands",
    )(*map(in_hbm, (stiff, rows, cols)), count, *map(in_hbm, (probes, diagonal, off_block)))


def eliminate(gram):
    count = gram.shape[0]
    start = jnp.concatenate([gram, (iota(gram.shape, 0) == iota(gram.shape, 1)).astype(F32)], 1)
    rows_done, pivots_done = [], []
    work = start
    for first in range(0, count, PANEL):
        row = iota((count - first, 1), 0)
        columns = [
            jnp.broadcast_to(work[:, j : j + 1], work.shape) for j in range(first, first + PANEL)
        ]
        for i in range(PANEL):
            factor = jnp.where(row > i, columns[i] * (1.0 / columns[i][i : i + 1, :]), 0.0)
            pivots_done.append(columns[i][i : i + 1, :])
            for k in range(i + 1, PANEL):
                columns[k] = columns[k] - factor * columns[k][i : i + 1, :]
            work = work - factor * work[i : i + 1, :]
        rows_done.append(work[:PANEL])
        work = work[PANEL:]
    work = jnp.concatenate(rows_done, axis=0)
    pivots = jnp.concatenate(pivots_done, axis=0)
    inverse = work[:, count:] * lax.rsqrt(pivots[:, :count])
    original = jnp.sum(
        jnp.where(iota(gram.shape, 0) == iota(gram.shape, 1), gram, 0.0), axis=1, keepdims=True
    )
    safe = jnp.where(pivots > SAFE_PIVOT * original, 1.0, 0.0)
    return inverse, jnp.min(safe, axis=0, keepdims=True)


def split(x):
    high = x.astype(BF16)
    return high, (x - high.astype(F32)).astype(BF16)


def unknown_weights(weight, tiles):
    return jnp.concatenate([weight[0:1, :], weight[1:2, :]] * (tiles // 2), axis=1)


def sketch(basis, weight, level, matrix, careful):
    total = basis.shape[1]
    step_weight = weight * (1.0 / SHIFT)

    def image_of(basis):
        scaled = basis * weight
        high, low = split(scaled)
        both = jnp.dot(
            jnp.concatenate([high, low], axis=0), matrix[...], preferred_element_type=F32
        )
        applied = both[: high.shape[0]] + both[high.shape[0] :] + level * scaled
        return basis - step_weight * applied

    def normaliser(image):
        return eliminate(dot_nt(image, image, HIGHEST) * (1.0 / total))

    def iteration(_, basis):
        image = image_of(basis)
        inverse, _ = normaliser(image)
        return jnp.dot(inverse, image, preferred_element_type=F32, precision=HIGHEST)

    if careful:
        image = image_of(lax.fori_loop(0, ITERS - 1, iteration, basis))
    else:
        image = basis
        for _ in range(ITERS):
            image = image_of(image)
    inverse, safe = normaliser(image)
    return image, inverse, safe


PLANE = 9
OWN = 4
PARTS = 16
PAYLOAD_ROWS = 16
ROW_GROUPS = 24
PAYLOAD_LANES = ROW_GROUPS * DEFL
BLOCK_GROUPS = PLANE * DEFL
END_GROUPS = 36


def plane_step(m):
    return m // 3 - 1, m % 3 - 1


def facing(m):
    return {-1: (1,), 0: (0, 1), 1: (0,)}[plane_step(m)[1]]


def end_group(m, y, c):
    before = sum(3 * len(facing(i)) for i in range(m))
    return before + 3 * facing(m).index(y) + c


def end_picker(y, half):
    row, lane = iota((PARTS, half), 0), iota((PARTS, half), 1)
    end, part = row // 8, row % 8
    hit = (part // 3 == y) & (part < 6) & (lane == (part % 3) * TILE + end * (TILE - 1))
    return hit.astype(BF16)


def payload_group(rows):
    group = DEFL + PARTS
    m, r = rows // group, rows % group
    first = jnp.zeros(rows.shape, jnp.int32)
    for i in range(1, PLANE):
        first = jnp.where(m == i, end_group(i, facing(i)[0], 0), first)
    low_y = jnp.where(m % 3 == 0, 1, 0)
    count = jnp.where(m % 3 == 1, 6, 3)
    end, part = (r - DEFL) // 8, (r - DEFL) % 8 - 3 * low_y
    used = (part >= 0) & (part < count)
    ends = jnp.where(used, BLOCK_GROUPS + end * END_GROUPS + first + part, -1)
    return jnp.where(r < DEFL, m * DEFL + r, ends)


def group_order(i):
    tiles = ROW_GROUPS * DEFL // TILE
    return i % tiles * (TILE // DEFL) + i // tiles


def line_tree():
    side = [(0, 5), (0, 2), (2, 1), (2, 3), (5, 4), (5, 6), (5, 7)]
    return side + [(-a, -b) for a, b in side] + [(5, 8)]


def exchange_kernel(
    careful,
    basis_ref, weight_ref, level_ref, matrix_ref,
    out_ref, defl_ref, safe_ref,
    field_ref, full, sides, line_slots, wide_ref, safe_x, safe_y, safe_z,
    send_sem, recv_sem, line_send, line_recv, x_send, x_recv, y_send, y_recv,
    z_send, z_recv,
):
    n_x, n_y, n_z = (lax.axis_size(a) for a in ("gx", "gy", "gz"))
    my_x, my_y, my_z = (lax.axis_index(a) for a in ("gx", "gy", "gz"))
    total = basis_ref.shape[1]
    tiles = total // TILE
    half = total // 2
    tree = line_tree()

    def device(m):
        step_x, step_y = plane_step(m)
        return (lax.rem(my_x + step_x + n_x, n_x), lax.rem(my_y + step_y + n_y, n_y), my_z)

    def line(step):
        return (my_x, my_y, lax.rem(my_z + step + n_z, n_z))

    def row_x(step):
        return (lax.rem(my_x + step, n_x), my_y, my_z)

    def row_y(step):
        return (my_x, lax.rem(my_y + step, n_y), my_z)

    neighbours = [m for m in range(PLANE) if m != OWN]
    barrier = pltpu.get_barrier_semaphore()
    for step in sorted(range(1, n_z), key=lambda step: -min(step, n_z - step)):
        pl.semaphore_signal(barrier, inc=1, device_id=line(step), device_id_type=MESH)
    others = [row_x(step) for step in range(2, n_x - 1)] + [row_y(step) for step in range(2, n_y - 1)]
    for there in others + [device(m) for m in neighbours]:
        pl.semaphore_signal(barrier, inc=1, device_id=there, device_id_type=MESH)

    weight = unknown_weights(weight_ref[...], tiles)
    image, inverse, safe = sketch(basis_ref[...], weight, level_ref[...], matrix_ref, careful)
    safe_x[0:1, :] = jnp.concatenate([safe, safe], axis=1)[:, :TILE]
    basis = jnp.dot(inverse, image, preferred_element_type=F32, precision=HIGHEST)
    kept = basis[:DEFL]
    weighted = (kept * weight).astype(BF16)
    for t in range(tiles):
        field_ref[t % 2, :, t // 2 * TILE : (t // 2 + 1) * TILE] = weighted[
            :, t * TILE : (t + 1) * TILE
        ]
    pl.semaphore_wait(barrier, len(others) + len(neighbours) + n_z - 1)

    slot = {m: i for i, m in enumerate(m for m in neighbours if plane_step(m)[1] != 0)}
    copies = []
    for m in neighbours:
        step_x, step_y = plane_step(m)
        back = PLANE - 1 - m
        if step_y == 0:
            source, target = field_ref, full.at[back // 3 // 2]
        else:
            source, target = field_ref.at[1 if step_y > 0 else 0], sides.at[slot[back]]
        copy = pltpu.make_async_remote_copy(
            src_ref=source,
            dst_ref=target,
            send_sem=send_sem.at[m],
            recv_sem=recv_sem.at[back],
            device_id=device(m),
            device_id_type=MESH,
        )
        copy.start()
        copies.append(copy)

    def spread_safe(rows, count, where, sends, recvs):
        out = []
        for step in range(1, count):
            copy = pltpu.make_async_remote_copy(
                src_ref=rows.at[pl.ds(0, 1)],
                dst_ref=rows.at[pl.ds(step, 1)],
                send_sem=sends.at[step],
                recv_sem=recvs.at[step],
                device_id=where(step),
                device_id_type=MESH,
            )
            copy.start()
            out.append(copy)
        return out

    safe_copies = spread_safe(safe_x, n_x, row_x, x_send, x_recv)

    for t in range(tiles):
        wide_ref[pl.ds(t, DEFL, stride=tiles), :] = kept[:, t * TILE : (t + 1) * TILE]
    defl_ref[...] = wide_ref[...].astype(BF16)
    applied = jnp.dot(weighted, matrix_ref[...], preferred_element_type=F32)
    applied = applied + level_ref[...] * weighted.astype(F32)
    high, low = split(applied)
    self_block = (dot_nt(weighted, high) + dot_nt(weighted, low)) * (1.0 / total)

    pick = [end_picker(y, half) for y in range(2)]
    own = [field_ref[y] for y in range(2)]
    stack = [[jnp.concatenate([-own[y], pick[z]], axis=0) for z in range(2)] for y in range(2)]
    rows = PLANE * (DEFL + PARTS)
    per_tile = TILE // DEFL
    groups = PAYLOAD_ROWS * ROW_GROUPS
    order = iota((groups, 1), 0)
    order = modulo(order, PAYLOAD_ROWS) * ROW_GROUPS + group_order(over(order, PAYLOAD_ROWS))
    arrange = (payload_group(iota((1, rows), 1)) == order).astype(BF16)
    lane, value = iota((DEFL, TILE), 1), iota((DEFL, TILE), 0)
    place = [(lane == value + v * DEFL).astype(BF16) for v in range(per_tile)]
    for copy in safe_copies:
        copy.wait_recv()
    safe_y[0:1, :] = jnp.min(safe_x[...], axis=0, keepdims=True)
    safe_copies += spread_safe(safe_y, n_y, row_y, y_send, y_recv)
    for copy in copies:
        copy.wait_recv()

    parts = []
    for m in range(PLANE):
        step_x, step_y = plane_step(m)
        if m == OWN:
            ends = dot_nt(pick[0], own[0]) + dot_nt(pick[1], own[1])
            parts.append(jnp.concatenate([self_block, ends], axis=0))
            continue
        if step_y == 0:
            side = m // 3 // 2
            block = dot_nt(stack[0][0], full[side, 0]) + dot_nt(stack[1][1], full[side, 1])
        elif step_y < 0:
            block = dot_nt(stack[0][1], sides[slot[m]])
        else:
            block = dot_nt(stack[1][0], sides[slot[m]])
        inside = True
        if step_x != 0:
            inside = my_x < n_x - 1 if step_x > 0 else my_x > 0
        if step_y != 0:
            inside = jnp.logical_and(inside, my_y < n_y - 1 if step_y > 0 else my_y > 0)
        parts.append(jnp.where(inside, block, 0.0))
    parts = jnp.concatenate(parts, axis=0).astype(BF16)

    sorted_rows = jnp.dot(arrange, parts, preferred_element_type=F32).astype(BF16)
    count = groups // per_tile
    flat = sum(
        jnp.dot(
            sorted_rows[v * count : (v + 1) * count], place[v], preferred_element_type=F32
        )
        for v in range(per_tile)
    ).astype(BF16)
    for i in range(ROW_GROUPS // per_tile):
        line_slots[my_z, :, i * TILE : (i + 1) * TILE] = flat[
            i * PAYLOAD_ROWS : (i + 1) * PAYLOAD_ROWS
        ]

    sign = 1 - 2 * lax.rem(my_x, 2)
    hops = {}

    def send(parent, child):
        owner = line_slots.at[lax.rem(my_z - sign * parent + n_z, n_z)]
        hop = pltpu.make_async_remote_copy(
            src_ref=owner,
            dst_ref=owner,
            send_sem=line_send.at[child + n_z // 2],
            recv_sem=line_recv.at[child + n_z // 2],
            device_id=line(sign * (child - parent)),
            device_id_type=MESH,
        )
        hop.start()
        hops[child] = hop

    for parent, child in tree:
        if parent == 0:
            send(parent, child)
    for copy in safe_copies[n_x - 1 :]:
        copy.wait_recv()
    safe_z[0:1, :] = jnp.min(safe_y[...], axis=0, keepdims=True)
    safe_copies_z = spread_safe(safe_z, n_z, line, z_send, z_recv)
    parents = [p for p in sorted({p for p, _ in tree}, key=abs) if p != 0]
    for p in parents:
        hops[p].wait_recv()
        for parent, child in tree:
            if parent == p:
                send(parent, child)
    for child, hop in hops.items():
        if child not in parents:
            hop.wait_recv()
    for copy in safe_copies_z:
        copy.wait_recv()
    for copy in copies + safe_copies + safe_copies_z + list(hops.values()):
        copy.wait_send()
    out_ref[...] = line_slots[...]
    safe_ref[...] = jnp.min(safe_z[...], axis=0, keepdims=True)


def exchange(basis, weight, level, matrix, sizes, careful):
    vmem = pl.BlockSpec(memory_space=pltpu.VMEM)
    dma = pltpu.SemaphoreType.DMA
    n_x, n_y, n_z = sizes
    total = basis.shape[1]
    payload = (n_z, PAYLOAD_ROWS, PAYLOAD_LANES)
    rows = DEFL * total // TILE
    return pl.pallas_call(
        functools.partial(exchange_kernel, careful),
        out_shape=(
            jax.ShapeDtypeStruct(payload, BF16),
            jax.ShapeDtypeStruct((rows, TILE), BF16),
            jax.ShapeDtypeStruct((1, TILE), F32),
        ),
        in_specs=[vmem] * 4,
        out_specs=(vmem, vmem, vmem),
        scratch_shapes=[
            pltpu.VMEM((2, DEFL, total // 2), BF16),
            pltpu.VMEM((2, 2, DEFL, total // 2), BF16),
            pltpu.VMEM((6, DEFL, total // 2), BF16),
            pltpu.VMEM(payload, BF16),
            pltpu.VMEM((rows, TILE), F32),
            pltpu.VMEM((n_x, TILE), F32),
            pltpu.VMEM((n_y, TILE), F32),
            pltpu.VMEM((n_z, TILE), F32),
            dma((PLANE,)),
            dma((PLANE,)),
            dma((n_z + 1,)),
            dma((n_z + 1,)),
            dma((n_x,)),
            dma((n_x,)),
            dma((n_y,)),
            dma((n_y,)),
            dma((n_z,)),
            dma((n_z,)),
        ],
        compiler_params=pltpu.CompilerParams(
            collective_id=2 if careful else 1,
            has_side_effects=True,
            vmem_limit_bytes=24 * 2**20,
        ),
        name="exchange_careful" if careful else "exchange",
    )(basis, weight, level, matrix)


def pair_index(m, step_z):
    flat = 3 * m + step_z + 1
    return flat if flat < 13 else flat - 1


def unpack_kernel(
    gathered_ref, kept_ref, self_hbm, pairs_hbm, defl_hbm, self_ref, pairs_ref, sem
):
    n_z = self_ref.shape[0]
    width = DEFL * DEFL
    stores = []

    def store(source, target):
        copy = pltpu.make_async_copy(source, target, sem.at[len(stores)])
        copy.start()
        stores.append(copy)

    def store_pair(index, block):
        pairs_ref[index] = block
        store(pairs_ref.at[index], pairs_hbm.at[index])

    store(kept_ref, defl_hbm)
    packed = gathered_ref[...]
    column = iota((1, n_z * PAYLOAD_ROWS), 1)

    def select(first, count, shift):
        index = iota((count * n_z, 1), 0)
        member = modulo(index, n_z) + shift
        inside = (member >= 0) & (member < n_z)
        wanted = jnp.where(inside, member * PAYLOAD_ROWS + first + over(index, n_z), -1)
        hit = (column == wanted).astype(BF16)
        return jnp.dot(hit, packed, preferred_element_type=F32)

    block_rows = BLOCK_GROUPS // ROW_GROUPS
    rows = select(0, block_rows, 0)
    for m in range(PLANE):
        pieces, group = [], m * DEFL
        while group < (m + 1) * DEFL:
            row, start = group // ROW_GROUPS, group % ROW_GROUPS
            stop = min(ROW_GROUPS, start + (m + 1) * DEFL - group)
            pieces.append(rows[row * n_z : (row + 1) * n_z, start * DEFL : stop * DEFL])
            group += stop - start
        block = jnp.concatenate(pieces, axis=1)
        if m == OWN:
            self_ref[...] = block
            store(self_ref, self_hbm)
        else:
            store_pair(pair_index(m, 0), block)

    per_tile = TILE // DEFL
    row_tiles = ROW_GROUPS // per_tile
    end_tiles = END_GROUPS // per_tile
    end_rows = 2 * END_GROUPS // ROW_GROUPS

    def tile_of(rows, number):
        row, i = number // row_tiles, number % row_tiles
        return rows[row * n_z : (row + 1) * n_z, i * TILE : (i + 1) * TILE]

    own_first = end_group(OWN, 0, 0) // per_tile
    own_count = end_group(OWN, 1, 2) // per_tile + 1 - own_first
    rows = select(block_rows, end_rows, 0).astype(BF16)
    own_tiles = jnp.concatenate(
        [tile_of(rows, end * end_tiles + own_first + i) for end in range(2) for i in range(own_count)],
        axis=0,
    )
    distance = iota((TILE, width), 0) - over(iota((TILE, width), 1), DEFL)
    own = []
    for v in range(per_tile):
        spread = jnp.where(distance == v * DEFL, -1.0, 0.0).astype(BF16)
        own.append(jnp.dot(own_tiles, spread, preferred_element_type=F32))

    def own_part(end, y, c):
        group = end_group(OWN, y, c)
        start = (end * own_count + group // per_tile - own_first) * n_z
        return own[group % per_tile][start : start + n_z]

    value, lane = iota((TILE, per_tile * TILE), 0), iota((TILE, per_tile * TILE), 1)
    repeat = (value == over(lane, TILE) * DEFL + modulo(lane, DEFL)).astype(BF16)
    for step_z in (-1, 1):
        their_end, own_end = (0, 1) if step_z > 0 else (1, 0)
        rows = select(block_rows, end_rows, step_z).astype(BF16)
        tiles = [tile_of(rows, their_end * end_tiles + i) for i in range(end_tiles)]
        theirs = jnp.dot(jnp.concatenate(tiles, axis=0), repeat, preferred_element_type=F32)
        for m in range(PLANE):
            step_y = plane_step(m)[1]
            pairs = [(0, 0), (1, 1)] if step_y == 0 else [(0, 1)] if step_y < 0 else [(1, 0)]
            total = None
            for own_y, their_y in pairs:
                for c in range(3):
                    group = end_group(m, their_y, c)
                    start, v = group // per_tile * n_z, group % per_tile
                    right = theirs[start : start + n_z, v * TILE : (v + 1) * TILE]
                    right = jnp.concatenate([right] * (width // TILE), axis=1)
                    term = own_part(own_end, own_y, c) * right
                    total = term if total is None else total + term
            store_pair(pair_index(m, step_z), total)
    for copy in stores:
        copy.wait()


def unpack(gathered, kept, n_z):
    vmem = pl.BlockSpec(memory_space=pltpu.VMEM)
    hbm = pl.BlockSpec(memory_space=pltpu.HBM)
    width = DEFL * DEFL
    pairs = 3 * PLANE - 1
    return pl.pallas_call(
        unpack_kernel,
        out_shape=(
            jax.ShapeDtypeStruct((n_z, width), F32),
            jax.ShapeDtypeStruct((pairs, n_z, width), F32),
            jax.ShapeDtypeStruct(kept.shape, kept.dtype),
        ),
        in_specs=[vmem, vmem],
        out_specs=(hbm, hbm, hbm),
        scratch_shapes=[
            pltpu.VMEM((n_z, width), F32),
            pltpu.VMEM((pairs, n_z, width), F32),
            pltpu.SemaphoreType.DMA((pairs + 2,)),
        ],
        compiler_params=pltpu.CompilerParams(vmem_limit_bytes=32 * 2**20),
        name="unpack",
    )(gathered.reshape(n_z * PAYLOAD_ROWS, PAYLOAD_LANES), kept)


def per_device(probes, stiffness, diag_tiles, off_tiles, off_rows, off_cols, off_count):
    sizes = tuple(lax.axis_size(a) for a in ("gx", "gy", "gz"))
    n_z = sizes[2]
    cell_shape = probes.shape[1:]
    weight, basis, level, matrix = sketch_operands(
        probes.reshape(-1, TILE),
        stiffness[0],
        diag_tiles[0, 0, 0],
        off_tiles[0, 0, 0],
        off_rows[0, 0, 0],
        off_cols[0, 0, 0],
        off_count[0, 0],
    )
    gathered, kept, safe = exchange(basis, weight, level, matrix, sizes, careful=False)

    def careful():
        again = exchange(basis, weight, level, matrix, sizes, careful=True)
        return unpack(again[0], again[1], n_z)

    coarse_self, coarse_pairs, deflation = lax.cond(
        safe[0, 0] > 0.5, lambda: unpack(gathered, kept, n_z), careful
    )
    return (
        deflation.reshape((DEFL,) + cell_shape),
        coarse_self[None, None],
        coarse_pairs.transpose(1, 0, 2)[None, None],
    )


def solution(mesh):
    placed = (
        P(None, None, "gx", "gy", "gz"),
        P("gx", "gy", "gz"),
        P("gx", "gy", "gz", None, None, None),
        P("gx", "gy", "gz", None, None, None),
        P("gx", "gy", "gz", None),
        P("gx", "gy", "gz", None),
        P("gx", "gy", "gz"),
    )
    return jax.shard_map(
        per_device,
        mesh=mesh,
        in_specs=placed,
        out_specs=(
            P(None, None, "gx", "gy", "gz"),
            P("gx", "gy", None, None),
            P("gx", "gy", None, None, None),
        ),
        check_vma=False,
    )
```

```python
import functools

import jax
import jax.numpy as jnp
from jax import lax
from jax.experimental import pallas as pl
from jax.experimental.pallas import tpu as pltpu
from jax.sharding import PartitionSpec as P

MESH = pl.DeviceIdType.MESH
F32 = jnp.float32
BF16 = jnp.bfloat16
HIGHEST = lax.Precision.HIGHEST

DEFL = 32
ITERS = 12
SHIFT = 8.0
TILE = 128
SAFE_PIVOT = 0.01
PANEL = 8


def iota(shape, dim):
    return lax.broadcasted_iota(jnp.int32, shape, dim)


def over(x, n):
    return x >> (n.bit_length() - 1) if n & (n - 1) == 0 else x // n


def modulo(x, n):
    return x & (n - 1) if n & (n - 1) == 0 else x % n


def dot_nt(a, b, precision=None):
    return lax.dot_general(
        a, b, (((1,), (1,)), ((), ())), preferred_element_type=F32, precision=precision
    )


def operands_kernel(
    stiff_hbm, rows_hbm, cols_hbm, count_hbm, probe_hbm, diag_hbm, off_hbm,
    weight_ref, basis_ref, level_ref, matrix_ref,
    got, stiff_ref, rows_ref, cols_ref, count_ref, key_ref, probe_ref, diag_ref, off_ref, wide, sums,
    send_sem, recv_sem, local_sem,
):
    sizes = [lax.axis_size(a) for a in ("gx", "gy", "gz")]
    here = [lax.axis_index(a) for a in ("gx", "gy", "gz")]
    slots, tiles = off_ref.shape[0], diag_ref.shape[0]
    faces = []
    for dim, size in enumerate(sizes):
        for step in (-1, 1):
            there = list(here)
            there[dim] = lax.rem(here[dim] + step + size, size)
            faces.append(tuple(there))
    barrier = pltpu.get_barrier_semaphore()
    for there in faces:
        pl.semaphore_signal(barrier, inc=1, device_id=there, device_id_type=MESH)
    loads = []
    for source, target in (
        (rows_hbm, rows_ref),
        (cols_hbm, cols_ref),
        (count_hbm, count_ref),
        (off_hbm, off_ref),
        (diag_hbm, diag_ref),
        (probe_hbm, probe_ref),
        (stiff_hbm, stiff_ref),
    ):
        load = pltpu.make_async_copy(source, target, local_sem.at[len(loads)])
        load.start()
        loads.append(load)
    pl.semaphore_wait(barrier, len(faces))
    copies = []
    for face, there in enumerate(faces):
        copy = pltpu.make_async_remote_copy(
            src_ref=stiff_hbm,
            dst_ref=got.at[face ^ 1],
            send_sem=send_sem.at[face],
            recv_sem=recv_sem.at[face ^ 1],
            device_id=there,
            device_id_type=MESH,
        )
        copy.start()
        copies.append(copy)

    for load in loads[:3]:
        load.wait()
    count = count_ref[0]
    for m in range(slots):
        key_ref[m] = jnp.where(m < count, rows_ref[m] * tiles + cols_ref[m], -1 - m)
    sums[slots] = jnp.zeros((TILE, TILE), F32)
    loads[3].wait()

    def add_tile(m, carry):
        key, before = key_ref[m], slots
        for other in range(slots - 1):
            before = jnp.where((other < m) & (key_ref[other] == key), other, before)
        sums[m] = off_ref[m].astype(F32) + sums[before]
        return carry

    lax.fori_loop(0, slots, add_tile, 0)

    def dense_block(place):
        last = slots
        for m in range(slots):
            last = jnp.where(key_ref[m] == place, m, last)
        return sums[last]

    loads[4].wait()
    eye = iota((TILE, TILE), 0) == iota((TILE, TILE), 1)
    for t in range(tiles):
        columns = slice(t * TILE, (t + 1) * TILE)
        for u in range(tiles):
            block = dense_block(t * tiles + u)
            if t == u:
                block = block + diag_ref[t].astype(F32)
                level_ref[:, columns] = jnp.sum(jnp.where(eye, block, 0.0), axis=0, keepdims=True)
                block = jnp.where(eye, 0.0, block)
            matrix_ref[u * TILE : (u + 1) * TILE, columns] = block.astype(BF16).T

    loads[5].wait()
    wide[...] = probe_ref[...].astype(F32)
    for t in range(tiles):
        basis_ref[:, t * TILE : (t + 1) * TILE] = wide[pl.ds(t, basis_ref.shape[0], stride=tiles), :]

    loads[6].wait()
    for copy in copies:
        copy.wait()
    zero = jnp.zeros(stiff_ref.shape, F32)
    stiff = stiff_ref[...]

    def face_value(face):
        dim, high = face // 2, face % 2
        inside = here[dim] < sizes[dim] - 1 if high else here[dim] > 0
        return jnp.where(inside, got[face], zero)

    total = face_value(1) + face_value(0)
    row = iota(stiff.shape, 0)
    y_low, y_high = face_value(2), face_value(3)
    total = total + jnp.where(row == 0, pltpu.roll(stiff, 1, 0), y_high[0:1, :])
    total = total + jnp.where(row == 1, pltpu.roll(stiff, 1, 0), y_low[1:2, :])
    lane = iota(stiff.shape, 1)
    z_low, z_high = face_value(4), face_value(5)
    width = stiff.shape[1]
    total = total + jnp.where(
        lane == width - 1, z_high[:, 0:1], pltpu.roll(stiff, width - 1, 1)
    )
    total = total + jnp.where(lane == 0, z_low[:, width - 1 : width], pltpu.roll(stiff, 1, 1))
    weight_ref[...] = stiff / (stiff + total / 6.0)


def in_hbm(x):
    return pltpu.with_memory_space_constraint(x, pltpu.HBM)


def sketch_operands(probes, stiff, diagonal, off_block, rows, cols, count):
    vmem = pl.BlockSpec(memory_space=pltpu.VMEM)
    hbm = pl.BlockSpec(memory_space=pltpu.HBM)
    dma = pltpu.SemaphoreType.DMA
    tiles, slots = diagonal.shape[0], off_block.shape[0]
    total = tiles * TILE
    return pl.pallas_call(
        operands_kernel,
        out_shape=(
            jax.ShapeDtypeStruct(stiff.shape, F32),
            jax.ShapeDtypeStruct((probes.shape[0] // tiles, total), F32),
            jax.ShapeDtypeStruct((1, total), F32),
            jax.ShapeDtypeStruct((total, total), BF16),
        ),
        in_specs=[hbm] * 7,
        out_specs=(vmem, vmem, vmem, vmem),
        scratch_shapes=[
            pltpu.VMEM((6,) + stiff.shape, F32),
            pltpu.VMEM(stiff.shape, F32),
            pltpu.SMEM(rows.shape, jnp.int32),
            pltpu.SMEM(cols.shape, jnp.int32),
            pltpu.SMEM(count.shape, jnp.int32),
            pltpu.SMEM(rows.shape, jnp.int32),
            pltpu.VMEM(probes.shape, BF16),
            pltpu.VMEM(diagonal.shape, BF16),
            pltpu.VMEM(off_block.shape, BF16),
            pltpu.VMEM(probes.shape, F32),
            pltpu.VMEM((slots + 1, TILE, TILE), F32),
            dma((6,)),
            dma((6,)),
            dma((7,)),
        ],
        compiler_params=pltpu.CompilerParams(
            collective_id=0, has_side_effects=True, vmem_limit_bytes=24 * 2**20
        ),
        name="sketch_operands",
    )(*map(in_hbm, (stiff, rows, cols)), count, *map(in_hbm, (probes, diagonal, off_block)))


def eliminate(gram):
    count = gram.shape[0]
    start = jnp.concatenate([gram, (iota(gram.shape, 0) == iota(gram.shape, 1)).astype(F32)], 1)
    rows_done, pivots_done = [], []
    work = start
    for first in range(0, count, PANEL):
        row = iota((count - first, 1), 0)
        columns = [
            jnp.broadcast_to(work[:, j : j + 1], work.shape) for j in range(first, first + PANEL)
        ]
        for i in range(PANEL):
            factor = jnp.where(row > i, columns[i] * (1.0 / columns[i][i : i + 1, :]), 0.0)
            pivots_done.append(columns[i][i : i + 1, :])
            for k in range(i + 1, PANEL):
                columns[k] = columns[k] - factor * columns[k][i : i + 1, :]
            work = work - factor * work[i : i + 1, :]
        rows_done.append(work[:PANEL])
        work = work[PANEL:]
    work = jnp.concatenate(rows_done, axis=0)
    pivots = jnp.concatenate(pivots_done, axis=0)
    inverse = work[:, count:] * lax.rsqrt(pivots[:, :count])
    original = jnp.sum(
        jnp.where(iota(gram.shape, 0) == iota(gram.shape, 1), gram, 0.0), axis=1, keepdims=True
    )
    safe = jnp.where(pivots > SAFE_PIVOT * original, 1.0, 0.0)
    return inverse, jnp.min(safe, axis=0, keepdims=True)


def split(x):
    high = x.astype(BF16)
    return high, (x - high.astype(F32)).astype(BF16)


def unknown_weights(weight, tiles):
    return jnp.concatenate([weight[0:1, :], weight[1:2, :]] * (tiles // 2), axis=1)


def sketch(basis, weight, level, matrix, careful):
    total = basis.shape[1]
    step_weight = weight * (1.0 / SHIFT)

    def image_of(basis):
        scaled = basis * weight
        high, low = split(scaled)
        both = jnp.dot(
            jnp.concatenate([high, low], axis=0), matrix[...], preferred_element_type=F32
        )
        applied = both[: high.shape[0]] + both[high.shape[0] :] + level * scaled
        return basis - step_weight * applied

    def normaliser(image):
        return eliminate(dot_nt(image, image, HIGHEST) * (1.0 / total))

    def iteration(_, basis):
        image = image_of(basis)
        inverse, _ = normaliser(image)
        return jnp.dot(inverse, image, preferred_element_type=F32, precision=HIGHEST)

    if careful:
        image = image_of(lax.fori_loop(0, ITERS - 1, iteration, basis))
    else:
        image = basis
        for _ in range(ITERS):
            image = image_of(image)
    inverse, safe = normaliser(image)
    return image, inverse, safe


PLANE = 9
OWN = 4
PARTS = 16
PAYLOAD_ROWS = 16
ROW_GROUPS = 24
PAYLOAD_LANES = ROW_GROUPS * DEFL
BLOCK_GROUPS = PLANE * DEFL
END_GROUPS = 36


def plane_step(m):
    return m // 3 - 1, m % 3 - 1


def facing(m):
    return {-1: (1,), 0: (0, 1), 1: (0,)}[plane_step(m)[1]]


def end_group(m, y, c):
    before = sum(3 * len(facing(i)) for i in range(m))
    return before + 3 * facing(m).index(y) + c


def end_picker(y, half):
    row, lane = iota((PARTS, half), 0), iota((PARTS, half), 1)
    end, part = row // 8, row % 8
    hit = (part // 3 == y) & (part < 6) & (lane == (part % 3) * TILE + end * (TILE - 1))
    return hit.astype(BF16)


def payload_group(rows):
    group = DEFL + PARTS
    m, r = rows // group, rows % group
    first = jnp.zeros(rows.shape, jnp.int32)
    for i in range(1, PLANE):
        first = jnp.where(m == i, end_group(i, facing(i)[0], 0), first)
    low_y = jnp.where(m % 3 == 0, 1, 0)
    count = jnp.where(m % 3 == 1, 6, 3)
    end, part = (r - DEFL) // 8, (r - DEFL) % 8 - 3 * low_y
    used = (part >= 0) & (part < count)
    ends = jnp.where(used, BLOCK_GROUPS + end * END_GROUPS + first + part, -1)
    return jnp.where(r < DEFL, m * DEFL + r, ends)


def group_order(i):
    tiles = ROW_GROUPS * DEFL // TILE
    return i % tiles * (TILE // DEFL) + i // tiles


def line_tree():
    side = [(0, 5), (0, 2), (2, 1), (2, 3), (5, 4), (5, 6), (5, 7)]
    return side + [(-a, -b) for a, b in side] + [(5, 8)]


def exchange_kernel(
    careful,
    basis_ref, weight_ref, level_ref, matrix_ref,
    out_ref, defl_ref, safe_ref,
    field_ref, full, sides, line_slots, wide_ref, safe_x, safe_y, safe_z,
    send_sem, recv_sem, line_send, line_recv, x_send, x_recv, y_send, y_recv,
    z_send, z_recv,
):
    n_x, n_y, n_z = (lax.axis_size(a) for a in ("gx", "gy", "gz"))
    my_x, my_y, my_z = (lax.axis_index(a) for a in ("gx", "gy", "gz"))
    total = basis_ref.shape[1]
    tiles = total // TILE
    half = total // 2
    tree = line_tree()

    def device(m):
        step_x, step_y = plane_step(m)
        return (lax.rem(my_x + step_x + n_x, n_x), lax.rem(my_y + step_y + n_y, n_y), my_z)

    def line(step):
        return (my_x, my_y, lax.rem(my_z + step + n_z, n_z))

    def row_x(step):
        return (lax.rem(my_x + step, n_x), my_y, my_z)

    def row_y(step):
        return (my_x, lax.rem(my_y + step, n_y), my_z)

    neighbours = [m for m in range(PLANE) if m != OWN]
    barrier = pltpu.get_barrier_semaphore()
    distances = sorted({abs(child - parent) for parent, child in tree}, reverse=True)
    for step in [sign * distance for distance in distances for sign in (-1, 1)]:
        pl.semaphore_signal(barrier, inc=1, device_id=line(step), device_id_type=MESH)
    others = [row_x(step) for step in range(2, n_x - 1)] + [row_y(step) for step in range(2, n_y - 1)]
    for there in others + [device(m) for m in neighbours]:
        pl.semaphore_signal(barrier, inc=1, device_id=there, device_id_type=MESH)

    weight = unknown_weights(weight_ref[...], tiles)
    image, inverse, safe = sketch(basis_ref[...], weight, level_ref[...], matrix_ref, careful)
    safe_x[0:1, :] = jnp.concatenate([safe, safe], axis=1)[:, :TILE]
    basis = jnp.dot(inverse, image, preferred_element_type=F32, precision=HIGHEST)
    kept = basis[:DEFL]
    weighted = (kept * weight).astype(BF16)
    for t in range(tiles):
        field_ref[t % 2, :, t // 2 * TILE : (t // 2 + 1) * TILE] = weighted[
            :, t * TILE : (t + 1) * TILE
        ]
    pl.semaphore_wait(barrier, len(others) + len(neighbours) + 2 * len(distances))

    slot = {m: i for i, m in enumerate(m for m in neighbours if plane_step(m)[1] != 0)}
    copies, arrival = [], {}
    for m in neighbours:
        step_x, step_y = plane_step(m)
        back = PLANE - 1 - m
        if step_y == 0:
            source, target = field_ref, full.at[back // 3 // 2]
        else:
            source, target = field_ref.at[1 if step_y > 0 else 0], sides.at[slot[back]]
        copy = pltpu.make_async_remote_copy(
            src_ref=source,
            dst_ref=target,
            send_sem=send_sem.at[m],
            recv_sem=recv_sem.at[back],
            device_id=device(m),
            device_id_type=MESH,
        )
        copy.start()
        copies.append(copy)
        arrival[back] = copy

    def spread_safe(rows, count, where, sends, recvs):
        out = []
        for step in range(1, count):
            copy = pltpu.make_async_remote_copy(
                src_ref=rows.at[pl.ds(0, 1)],
                dst_ref=rows.at[pl.ds(step, 1)],
                send_sem=sends.at[step],
                recv_sem=recvs.at[step],
                device_id=where(step),
                device_id_type=MESH,
            )
            copy.start()
            out.append(copy)
        return out

    safe_copies = spread_safe(safe_x, n_x, row_x, x_send, x_recv)

    for t in range(tiles):
        wide_ref[pl.ds(t, DEFL, stride=tiles), :] = kept[:, t * TILE : (t + 1) * TILE]
    defl_ref[...] = wide_ref[...].astype(BF16)
    applied = jnp.dot(weighted, matrix_ref[...], preferred_element_type=F32)
    applied = applied + level_ref[...] * weighted.astype(F32)
    high, low = split(applied)
    self_block = (dot_nt(weighted, high) + dot_nt(weighted, low)) * (1.0 / total)

    pick = [end_picker(y, half) for y in range(2)]
    own = [field_ref[y] for y in range(2)]
    stack = [[jnp.concatenate([-own[y], pick[z]], axis=0) for z in range(2)] for y in range(2)]
    rows = PLANE * (DEFL + PARTS)
    per_tile = TILE // DEFL
    groups = PAYLOAD_ROWS * ROW_GROUPS
    order = iota((groups, 1), 0)
    order = modulo(order, PAYLOAD_ROWS) * ROW_GROUPS + group_order(over(order, PAYLOAD_ROWS))
    arrange = (payload_group(iota((1, rows), 1)) == order).astype(BF16)
    lane, value = iota((DEFL, TILE), 1), iota((DEFL, TILE), 0)
    place = [(lane == value + v * DEFL).astype(BF16) for v in range(per_tile)]
    blocks = {}
    ends = dot_nt(pick[0], own[0]) + dot_nt(pick[1], own[1])
    blocks[OWN] = jnp.concatenate([self_block, ends], axis=0)
    for copy in safe_copies:
        copy.wait_recv()
    safe_y[0:1, :] = jnp.min(safe_x[...], axis=0, keepdims=True)
    safe_copies += spread_safe(safe_y, n_y, row_y, y_send, y_recv)
    for m in sorted(neighbours, key=lambda m: sum(map(abs, plane_step(m)))):
        step_x, step_y = plane_step(m)
        arrival[m].wait_recv()
        if step_y == 0:
            side = m // 3 // 2
            block = dot_nt(stack[0][0], full[side, 0]) + dot_nt(stack[1][1], full[side, 1])
        elif step_y < 0:
            block = dot_nt(stack[0][1], sides[slot[m]])
        else:
            block = dot_nt(stack[1][0], sides[slot[m]])
        inside = True
        if step_x != 0:
            inside = my_x < n_x - 1 if step_x > 0 else my_x > 0
        if step_y != 0:
            inside = jnp.logical_and(inside, my_y < n_y - 1 if step_y > 0 else my_y > 0)
        blocks[m] = jnp.where(inside, block, 0.0)
    parts = jnp.concatenate([blocks[m] for m in range(PLANE)], axis=0).astype(BF16)

    sorted_rows = jnp.dot(arrange, parts, preferred_element_type=F32).astype(BF16)
    count = groups // per_tile
    flat = sum(
        jnp.dot(
            sorted_rows[v * count : (v + 1) * count], place[v], preferred_element_type=F32
        )
        for v in range(per_tile)
    ).astype(BF16)
    for i in range(ROW_GROUPS // per_tile):
        line_slots[my_z, :, i * TILE : (i + 1) * TILE] = flat[
            i * PAYLOAD_ROWS : (i + 1) * PAYLOAD_ROWS
        ]

    sign = 1 - 2 * lax.rem(my_x, 2)
    parents = sorted({parent for parent, _ in tree} - {0}, key=abs)

    def send(slots, parent, sends, recvs):
        hops = {}
        for start, child in tree:
            if start != parent:
                continue
            owner = slots.at[pl.ds(lax.rem(my_z - sign * parent + n_z, n_z), 1)]
            hops[child] = pltpu.make_async_remote_copy(
                src_ref=owner,
                dst_ref=owner,
                send_sem=sends.at[child + n_z // 2],
                recv_sem=recvs.at[child + n_z // 2],
                device_id=line(sign * (child - parent)),
                device_id_type=MESH,
            )
            hops[child].start()
        return hops

    hops = send(line_slots, 0, line_send, line_recv)
    for copy in safe_copies[n_x - 1 :]:
        copy.wait_recv()
    safe_z[pl.ds(my_z, 1), :] = jnp.min(safe_y[...], axis=0, keepdims=True)
    safe_hops = send(safe_z, 0, z_send, z_recv)
    for parent in parents:
        hops[parent].wait_recv()
        hops.update(send(line_slots, parent, line_send, line_recv))
    for parent in parents:
        safe_hops[parent].wait_recv()
        safe_hops.update(send(safe_z, parent, z_send, z_recv))
    for copies_of in (hops, safe_hops):
        for child, copy in copies_of.items():
            if child not in parents:
                copy.wait_recv()
    for copy in copies + safe_copies + list(hops.values()) + list(safe_hops.values()):
        copy.wait_send()
    out_ref[...] = line_slots[...]
    safe_ref[...] = jnp.min(safe_z[...], axis=0, keepdims=True)


def exchange(basis, weight, level, matrix, sizes, careful):
    vmem = pl.BlockSpec(memory_space=pltpu.VMEM)
    dma = pltpu.SemaphoreType.DMA
    n_x, n_y, n_z = sizes
    total = basis.shape[1]
    payload = (n_z, PAYLOAD_ROWS, PAYLOAD_LANES)
    rows = DEFL * total // TILE
    return pl.pallas_call(
        functools.partial(exchange_kernel, careful),
        out_shape=(
            jax.ShapeDtypeStruct(payload, BF16),
            jax.ShapeDtypeStruct((rows, TILE), BF16),
            jax.ShapeDtypeStruct((1, TILE), F32),
        ),
        in_specs=[vmem] * 4,
        out_specs=(vmem, vmem, vmem),
        scratch_shapes=[
            pltpu.VMEM((2, DEFL, total // 2), BF16),
            pltpu.VMEM((2, 2, DEFL, total // 2), BF16),
            pltpu.VMEM((6, DEFL, total // 2), BF16),
            pltpu.VMEM(payload, BF16),
            pltpu.VMEM((rows, TILE), F32),
            pltpu.VMEM((n_x, TILE), F32),
            pltpu.VMEM((n_y, TILE), F32),
            pltpu.VMEM((n_z, TILE), F32),
            dma((PLANE,)),
            dma((PLANE,)),
            dma((n_z + 1,)),
            dma((n_z + 1,)),
            dma((n_x,)),
            dma((n_x,)),
            dma((n_y,)),
            dma((n_y,)),
            dma((n_z + 1,)),
            dma((n_z + 1,)),
        ],
        compiler_params=pltpu.CompilerParams(
            collective_id=2 if careful else 1,
            has_side_effects=True,
            vmem_limit_bytes=24 * 2**20,
        ),
        name="exchange_careful" if careful else "exchange",
    )(basis, weight, level, matrix)


def pair_index(m, step_z):
    flat = 3 * m + step_z + 1
    return flat if flat < 13 else flat - 1


def unpack_kernel(
    gathered_ref, kept_ref, self_hbm, pairs_hbm, defl_hbm, self_ref, pairs_ref, sem
):
    n_z = self_ref.shape[0]
    width = DEFL * DEFL
    stores = []

    def store(source, target):
        copy = pltpu.make_async_copy(source, target, sem.at[len(stores)])
        copy.start()
        stores.append(copy)

    def store_pair(index, block):
        pairs_ref[index] = block
        store(pairs_ref.at[index], pairs_hbm.at[index])

    store(kept_ref, defl_hbm)
    packed = gathered_ref[...]
    column = iota((1, n_z * PAYLOAD_ROWS), 1)

    def hits(first, count, shift):
        index = iota((count * n_z, 1), 0)
        member = modulo(index, n_z) + shift
        inside = (member >= 0) & (member < n_z)
        wanted = jnp.where(inside, member * PAYLOAD_ROWS + first + over(index, n_z), -1)
        return (column == wanted).astype(BF16)

    block_rows = BLOCK_GROUPS // ROW_GROUPS
    end_rows = 2 * END_GROUPS // ROW_GROUPS
    wanted = [hits(0, block_rows, 0)] + [hits(block_rows, end_rows, step) for step in (0, -1, 1)]
    selected = jnp.dot(
        jnp.concatenate(wanted, axis=0), packed, preferred_element_type=F32
    )
    rows = selected[: block_rows * n_z]

    def ends_of(i):
        start = (block_rows + i * end_rows) * n_z
        return selected[start : start + end_rows * n_z].astype(BF16)

    for m in range(PLANE):
        pieces, group = [], m * DEFL
        while group < (m + 1) * DEFL:
            row, start = group // ROW_GROUPS, group % ROW_GROUPS
            stop = min(ROW_GROUPS, start + (m + 1) * DEFL - group)
            pieces.append(rows[row * n_z : (row + 1) * n_z, start * DEFL : stop * DEFL])
            group += stop - start
        block = jnp.concatenate(pieces, axis=1)
        if m == OWN:
            self_ref[...] = block
            store(self_ref, self_hbm)
        else:
            store_pair(pair_index(m, 0), block)

    per_tile = TILE // DEFL
    row_tiles = ROW_GROUPS // per_tile
    end_tiles = END_GROUPS // per_tile

    def tile_of(rows, number):
        row, i = number // row_tiles, number % row_tiles
        return rows[row * n_z : (row + 1) * n_z, i * TILE : (i + 1) * TILE]

    own_first = end_group(OWN, 0, 0) // per_tile
    own_count = end_group(OWN, 1, 2) // per_tile + 1 - own_first
    rows = ends_of(0)
    own_tiles = jnp.concatenate(
        [tile_of(rows, end * end_tiles + own_first + i) for end in range(2) for i in range(own_count)],
        axis=0,
    )
    distance = iota((TILE, width), 0) - over(iota((TILE, width), 1), DEFL)
    own = []
    for v in range(per_tile):
        spread = jnp.where(distance == v * DEFL, -1.0, 0.0).astype(BF16)
        own.append(jnp.dot(own_tiles, spread, preferred_element_type=F32))

    def own_part(end, y, c):
        group = end_group(OWN, y, c)
        start = (end * own_count + group // per_tile - own_first) * n_z
        return own[group % per_tile][start : start + n_z]

    value, lane = iota((TILE, per_tile * TILE), 0), iota((TILE, per_tile * TILE), 1)
    repeat = (value == over(lane, TILE) * DEFL + modulo(lane, DEFL)).astype(BF16)
    for step_z in (-1, 1):
        their_end, own_end = (0, 1) if step_z > 0 else (1, 0)
        rows = ends_of(1 if step_z < 0 else 2)
        tiles = [tile_of(rows, their_end * end_tiles + i) for i in range(end_tiles)]
        theirs = jnp.dot(jnp.concatenate(tiles, axis=0), repeat, preferred_element_type=F32)
        for m in range(PLANE):
            step_y = plane_step(m)[1]
            pairs = [(0, 0), (1, 1)] if step_y == 0 else [(0, 1)] if step_y < 0 else [(1, 0)]
            total = None
            for own_y, their_y in pairs:
                for c in range(3):
                    group = end_group(m, their_y, c)
                    start, v = group // per_tile * n_z, group % per_tile
                    right = theirs[start : start + n_z, v * TILE : (v + 1) * TILE]
                    right = jnp.concatenate([right] * (width // TILE), axis=1)
                    term = own_part(own_end, own_y, c) * right
                    total = term if total is None else total + term
            store_pair(pair_index(m, step_z), total)
    for copy in stores:
        copy.wait()


def unpack(gathered, kept, n_z):
    vmem = pl.BlockSpec(memory_space=pltpu.VMEM)
    hbm = pl.BlockSpec(memory_space=pltpu.HBM)
    width = DEFL * DEFL
    pairs = 3 * PLANE - 1
    return pl.pallas_call(
        unpack_kernel,
        out_shape=(
            jax.ShapeDtypeStruct((n_z, width), F32),
            jax.ShapeDtypeStruct((pairs, n_z, width), F32),
            jax.ShapeDtypeStruct(kept.shape, kept.dtype),
        ),
        in_specs=[vmem, vmem],
        out_specs=(hbm, hbm, hbm),
        scratch_shapes=[
            pltpu.VMEM((n_z, width), F32),
            pltpu.VMEM((pairs, n_z, width), F32),
            pltpu.SemaphoreType.DMA((pairs + 2,)),
        ],
        compiler_params=pltpu.CompilerParams(vmem_limit_bytes=32 * 2**20),
        name="unpack",
    )(gathered.reshape(n_z * PAYLOAD_ROWS, PAYLOAD_LANES), kept)


def per_device(probes, stiffness, diag_tiles, off_tiles, off_rows, off_cols, off_count):
    sizes = tuple(lax.axis_size(a) for a in ("gx", "gy", "gz"))
    n_z = sizes[2]
    cell_shape = probes.shape[1:]
    weight, basis, level, matrix = sketch_operands(
        probes.reshape(-1, TILE),
        stiffness[0],
        diag_tiles[0, 0, 0],
        off_tiles[0, 0, 0],
        off_rows[0, 0, 0],
        off_cols[0, 0, 0],
        off_count[0, 0],
    )
    gathered, kept, safe = exchange(basis, weight, level, matrix, sizes, careful=False)

    def careful():
        again = exchange(basis, weight, level, matrix, sizes, careful=True)
        return unpack(again[0], again[1], n_z)

    coarse_self, coarse_pairs, deflation = lax.cond(
        safe[0, 0] > 0.5, lambda: unpack(gathered, kept, n_z), careful
    )
    return (
        deflation.reshape((DEFL,) + cell_shape),
        coarse_self[None, None],
        coarse_pairs.transpose(1, 0, 2)[None, None],
    )


def solution(mesh):
    placed = (
        P(None, None, "gx", "gy", "gz"),
        P("gx", "gy", "gz"),
        P("gx", "gy", "gz", None, None, None),
        P("gx", "gy", "gz", None, None, None),
        P("gx", "gy", "gz", None),
        P("gx", "gy", "gz", None),
        P("gx", "gy", "gz"),
    )
    return jax.shard_map(
        per_device,
        mesh=mesh,
        in_specs=placed,
        out_specs=(
            P(None, None, "gx", "gy", "gz"),
            P("gx", "gy", None, None),
            P("gx", "gy", None, None, None),
        ),
        check_vma=False,
    )
```
